32 devices in a mesh: groups: 2 (over x), replica: 8 (over z, y), tensor: 2 (over core).
Axes of the slice: x: 2, y: 2, z: 4, core: 2. Of those that a mesh axis runs over, the one named last changes fastest.
Arguments:
- queries: bfloat16 [512, 8192], P(('groups', 'replica'), 'tensor'), parts along dimension 0, may hold values from -32 to 32
- fresh_key_rows: bfloat16 [512, 1024], P(('groups', 'replica'), 'tensor'), parts along dimension 0, may hold values from -8 to 8
- fresh_value_rows: bfloat16 [512, 1024], P(('groups', 'replica'), 'tensor'), parts along dimension 0, may hold values from -6 to 6
- paged_key_store: bfloat16 [2048, 16, 1024], P(('groups', 'replica'), None, 'tensor'), parts along dimension 0, may hold values from -8 to 8
- paged_value_store: bfloat16 [2048, 16, 1024], P(('groups', 'replica'), None, 'tensor'), parts along dimension 0, may hold values from -6 to 6
- page_table: int32 [512, 4], P(('groups', 'replica')), parts along dimension 0, may hold values from 0 to 127, as said below
- parent_replica: int32 [512, 1], P(('groups', 'replica')), parts along dimension 0, may hold values from 0 to 7; in each aligned block of 32 rows (0 to 31, 32 to 63, ...) at most 8 rows name the same one
- parent_slot: int32 [512, 1], P(('groups', 'replica')), parts along dimension 0, may hold values from 0 to 31
- context_length: int32 [512], P(('groups', 'replica')), parts along dimension 0, may hold values from 1 to 64, 4096 in all
- reward_probe: bfloat16 [8192], P('tensor'), may hold values from -0.0625 to 0.0625
Outputs:
- attended: bfloat16 [512, 8192], P(('groups', 'replica'), 'tensor'), parts along dimension 0
- reward: float32 [512], P(('groups', 'replica')), parts along dimension 0
The draws below stay inside these ranges and needn't reach their ends.
There are 2 independent parts, one for each index of `groups`. The reference program is written for one: setup_inputs(seed, part) draws one part's arguments, and reference() takes and returns one part's arrays. A program takes and returns all parts, laid end to end along the dimension named above; an argument that names none is the same for every part. Nothing has to cross between parts.
Inputs may be any that keep to these rules, and one draw needn't show every extreme that they name: `parent_replica`: within the rows of one replica no replica is named more than 8 times. `page_table`: the rows of one replica together name each of its 128 pool pages once.
All inputs are finite; a program needn't handle non-finite values. No bound on the sum of `context_length` on one device may be relied on, other than what follows from the above.
Results may differ from the reference program's by a relative error of at most 0.0033.
Values may be sent and summed in bfloat16 or wider, within the bound.
No kernel may reach another device: no remote copies, remote signals or barrier semaphores. Data moves between devices by JAX's collectives and lax.ppermute only.
A program may use at most 64 MiB of HBM per device.

```python
import math
import jax
import jax.numpy as jnp
import numpy as np
from jax import lax

QUERY_HEADS = 64
KEY_VALUE_HEADS = 8
HEAD_SIZE = 128
LEAF_ROWS = 32
PAGES_PER_ROW = 4
PAGE_POSITIONS = 16
MOST = 8
LEAF_ROWS_TOTAL = 256
POOL_PAGE_COUNT = 1024
N_REPLICA = 8


def draw_queries(key, part):
    key = jax.random.fold_in(key, 11)
    random_jitter = jnp.clip(jax.random.normal(key, (LEAF_ROWS_TOTAL, QUERY_HEADS * HEAD_SIZE), jnp.float32), -6.0, 6.0)
    final_output = random_jitter
    return final_output.astype(jnp.bfloat16)


def draw_fresh_key_rows(key, part):
    key = jax.random.fold_in(key, 12)
    random_jitter = jnp.clip(jax.random.normal(key, (LEAF_ROWS_TOTAL, KEY_VALUE_HEADS * HEAD_SIZE), jnp.float32), -6.0, 6.0)
    final_output = random_jitter
    return final_output.astype(jnp.bfloat16)


def draw_paged_key_store(key, part):
    key = jax.random.fold_in(key, 13)
    random_jitter = jnp.clip(jax.random.normal(key, (POOL_PAGE_COUNT, PAGE_POSITIONS, KEY_VALUE_HEADS * HEAD_SIZE), jnp.float32), -6.0, 6.0)
    final_output = random_jitter
    return final_output.astype(jnp.bfloat16)


def draw_page_table(key, part):
    key = jax.random.fold_in(key, 14)
    keys_all = jax.random.split(key, N_REPLICA)
    orders = jax.vmap(lambda single: jax.random.permutation(single, LEAF_ROWS * PAGES_PER_ROW))(keys_all)
    return orders.reshape(LEAF_ROWS_TOTAL, PAGES_PER_ROW).astype(jnp.int32)


def place_ends(values, rng, smallest, top_value):
    longest = values.shape.index(max(values.shape))
    spots = []
    for shift in (0, 1):
        where = [jax.random.randint(jax.random.fold_in(rng, axis), (), 0, length) for axis, length in enumerate(values.shape)]
        where[longest] = (where[longest] + shift) % values.shape[longest]
        spots.append(tuple(where))
    return values.at[spots[0]].set(smallest).at[spots[1]].set(top_value)


def steps_of(key, extent, cuts, low, largest):
    gain = 1.0
    for position, shards_of in cuts:
        steps = jax.random.uniform(jax.random.fold_in(jax.random.fold_in(key, 6), position), (shards_of,), jnp.float32, low / len(cuts), largest / len(cuts))
        gain = gain * jnp.repeat(jnp.exp(steps), extent[position] // shards_of).reshape((-1,) + (1,) * (len(extent) - 1 - position))
    return gain


def length_profile(number_of, total, limit, slope):
    portions = [(1 << 20) // math.isqrt(standing ** slope) + 1 for standing in range(2, number_of + 1)]
    spare, given = total - limit - (number_of - 1), [1] * (number_of - 1)
    while spare > 0:
        movable = [i for i in range(number_of - 1) if given[i] < limit]
        mass, left = sum([portions[i] for i in movable]), spare
        for i in movable:
            extra = min(limit - given[i], max(1, left * portions[i] // mass), spare)
            given[i] = given[i] + extra
            spare = spare - extra
    return np.array([limit] + given)


def ragged(key, number_of, total, most, skew):
    if number_of == 2:
        one = jax.random.randint(key, (), max(1, total - most), min(most, total - 1) + 1)
        return jnp.stack([one, total - one])
    sizes = jnp.asarray(length_profile(number_of, total, most, skew), jnp.int32)
    twos = (number_of - 1) // 2
    giver, sink = sizes[1:1 + 2 * twos:2], sizes[2:2 + 2 * twos:2]
    room = jnp.minimum(giver - 1, most - sink)
    moved = jax.random.randint(jax.random.fold_in(key, 1), (twos,), 0, 1 << 20) % (room + 1)
    sizes = sizes.at[1:1 + 2 * twos:2].set(giver - moved).at[2:2 + 2 * twos:2].set(sink + moved)
    return sizes[jax.random.permutation(jax.random.fold_in(key, 2), number_of)]


def shared_out(stream_key, own, number, rows, number_of, top, limit, lean):
    ranking = jax.random.permutation(stream_key, number_of)
    heavy_load, usual = load_shares(number_of, rows * top, limit, lean, True), load_shares(number_of, rows * top, limit, lean, False)
    places = jnp.arange(number_of)

    def named(tallies, offset_by):
        used = int((tallies > 0).sum())
        fixed = max(1, used // 4)
        shifted = fixed + (places - fixed + offset_by * (used - fixed)) % max(1, number_of - fixed)
        return jnp.zeros((number_of,), jnp.int32).at[ranking[jnp.where(places < fixed, places, shifted)]].set(jnp.asarray(tallies, jnp.int32))

    tallies = jnp.where(number % 4 == 0, named(heavy_load, number // 4), named(usual, number - number // 4 - 1))
    mixed = jax.random.permutation(jax.random.fold_in(own, 3), number_of)
    source_of, sink = mixed[0:number_of // 2 * 2:2], mixed[1:number_of // 2 * 2:2]
    room = jnp.minimum(tallies[source_of] - 1, limit - tallies[sink]) // 2
    room = jnp.where((source_of == ranking[0]) | (sink == ranking[0]) | (tallies[sink] == 0), 0, jnp.maximum(room, 0))
    shifted = jax.random.randint(jax.random.fold_in(own, 4), (number_of // 2,), 0, 1 << 20) % (room + 1)
    tallies = tallies.at[source_of].add(-shifted).at[sink].add(shifted)
    labels = jnp.searchsorted(jnp.cumsum(tallies), jnp.arange(rows * top), side="right").astype(jnp.int32)
    table = labels.reshape(top, rows).T
    table = table[jax.random.permutation(jax.random.fold_in(own, 1), rows)]
    offset_by = jax.random.randint(jax.random.fold_in(own, 2), (rows, 1), 0, top)
    return jnp.take_along_axis(table, (jnp.arange(top)[None, :] + offset_by) % top, axis=1)


def load_shares(count, total, reach, slope, full):
    weights = [(1 << 20) // math.isqrt(standing ** slope) + 1 for standing in range(1, count + 1)]
    largest = reach if full else min(reach, max(-(-total // count), total * weights[0] // sum(weights)))
    least = 1 if total - largest >= count - 1 else 0
    given, spare = [largest] + [least] * (count - 1), total - largest - least * (count - 1)
    while spare > 0:
        movable = [i for i in range(1, count) if given[i] < largest] or [i for i in range(1, count) if given[i] < reach]
        pool, remaining = sum([weights[i] for i in movable]), spare
        for i in movable:
            more = min(reach - given[i], max(1, remaining * weights[i] // pool), spare)
            given[i] = given[i] + more
            spare = spare - more
    return np.array(given)


def gaussian(stream_key, extent, width, bound, cuts=(), kind=jnp.bfloat16):
    level = steps_of(stream_key, extent, cuts, -0.22, 0.18) if cuts else 1.0
    result = jax.random.normal(stream_key, extent, jnp.float32) * width * level
    return jnp.minimum(jnp.maximum(result, -bound), bound).astype(kind)


def setup_inputs(seed: int = 0, part: int = 0) -> dict:
    seeds = jax.random.split(jax.random.key(seed), 11)
    part_keys = jax.random.split(jax.random.fold_in(seeds[10], part), 11)
    queries = draw_queries(jax.random.fold_in(jax.random.fold_in(seeds[10], part), 71), part)
    fresh_key_rows = draw_fresh_key_rows(jax.random.fold_in(jax.random.fold_in(seeds[10], part), 71), part)
    fresh_value_rows = gaussian(part_keys[2], (LEAF_ROWS_TOTAL, KEY_VALUE_HEADS * HEAD_SIZE), 1.0, 6.0, ((0, 8), (1, 2)))
    paged_key_store = draw_paged_key_store(jax.random.fold_in(jax.random.fold_in(seeds[10], part), 71), part)
    paged_value_store = gaussian(part_keys[4], (POOL_PAGE_COUNT, PAGE_POSITIONS, KEY_VALUE_HEADS * HEAD_SIZE), 1.0, 6.0, ((0, 8), (2, 2)))
    page_table = draw_page_table(jax.random.fold_in(jax.random.fold_in(seeds[10], part), 71), part)
    parent_replica_keys = jax.random.split(jax.random.fold_in(part_keys[6], 1), LEAF_ROWS_TOTAL // LEAF_ROWS)
    parent_replica_turns = jax.random.permutation(jax.random.fold_in(part_keys[6], 3), LEAF_ROWS_TOTAL // LEAF_ROWS)
    parent_replica = jax.vmap(lambda own, number: shared_out(jax.random.fold_in(part_keys[6], 2), own, number, LEAF_ROWS, N_REPLICA, 1, MOST, 2))(parent_replica_keys, parent_replica_turns).reshape((LEAF_ROWS_TOTAL, 1))
    parent_slot = place_ends(jax.random.randint(part_keys[7], (LEAF_ROWS_TOTAL, 1), 0, LEAF_ROWS), jax.random.fold_in(part_keys[7], 1), 0, LEAF_ROWS - 1).astype(jnp.int32)
    context_length = ragged(part_keys[8], LEAF_ROWS_TOTAL, LEAF_ROWS_TOTAL * PAGES_PER_ROW * PAGE_POSITIONS // 4, PAGES_PER_ROW * PAGE_POSITIONS, 2).astype(jnp.int32)
    reward_probe = gaussian(seeds[9], (QUERY_HEADS * HEAD_SIZE,), (QUERY_HEADS * HEAD_SIZE) ** -0.5, 0.0625, ((0, 2),))
    return dict(queries=queries, fresh_key_rows=fresh_key_rows, fresh_value_rows=fresh_value_rows, paged_key_store=paged_key_store, paged_value_store=paged_value_store, page_table=page_table, parent_replica=parent_replica, parent_slot=parent_slot, context_length=context_length, reward_probe=reward_probe)


masked_score = -1e30


def attend(query_rows, own_key, own_value, cached_key_rows, cached_value_rows, lengths):
    batch = query_rows.shape[0]
    key_span = cached_key_rows.shape[1]
    key_heads = own_key.shape[-1] // HEAD_SIZE
    group_size = query_rows.shape[-1] // own_key.shape[-1]
    scaling = 1.0 / (HEAD_SIZE ** 0.5)
    query_four = query_rows.reshape(batch, key_heads, group_size, HEAD_SIZE).astype(jnp.float32)
    keys_four = cached_key_rows.reshape(batch, key_span, key_heads, HEAD_SIZE).astype(jnp.float32)
    values_four = cached_value_rows.reshape(batch, key_span, key_heads, HEAD_SIZE).astype(jnp.float32)
    own_keys = own_key.reshape(batch, key_heads, HEAD_SIZE).astype(jnp.float32)
    own_values = own_value.reshape(batch, key_heads, HEAD_SIZE).astype(jnp.float32)
    scores = jnp.einsum("bgqd,btgd->bgqt", query_four, keys_four) * scaling
    own_score = jnp.einsum("bgqd,bgd->bgq", query_four, own_keys) * scaling
    visible = (jnp.arange(key_span, dtype=jnp.int32)[None, :] < lengths[:, None])[:, None, None, :]
    scores = jnp.where(visible, scores, masked_score)
    peak = jnp.maximum(jnp.max(scores, axis=-1), own_score)
    weights = jnp.where(visible, jnp.exp(scores - peak[..., None]), 0.0)
    own_weight = jnp.exp(own_score - peak)
    denominator = jnp.sum(weights, axis=-1) + own_weight
    rounded = weights.astype(jnp.bfloat16).astype(jnp.float32)
    own_rounded = own_weight.astype(jnp.bfloat16).astype(jnp.float32)
    numerator = jnp.einsum("bgqt,btgd->bgqd", rounded, values_four)
    numerator = numerator + own_rounded[..., None] * own_values[:, :, None, :]
    final_output = numerator / denominator[..., None]
    return final_output.reshape(batch, -1).astype(jnp.bfloat16)


def reference(queries, fresh_key_rows, fresh_value_rows, paged_key_store, paged_value_store, page_table, parent_replica, parent_slot, context_length, reward_probe):
    parent_rep = parent_replica[:, 0].astype(jnp.int32)
    parent = parent_rep * LEAF_ROWS + parent_slot[:, 0].astype(jnp.int32)
    page_numbers = (page_table[parent] + (parent_rep * (LEAF_ROWS * PAGES_PER_ROW))[:, None]).astype(jnp.int32)

    def attend_block(pieces):
        query_rows, own_key, own_value, row_page_lists, lengths = pieces
        cached_key_rows = paged_key_store[row_page_lists].reshape(row_page_lists.shape[0], PAGES_PER_ROW * PAGE_POSITIONS, KEY_VALUE_HEADS * HEAD_SIZE)
        cached_value_rows = paged_value_store[row_page_lists].reshape(row_page_lists.shape[0], PAGES_PER_ROW * PAGE_POSITIONS, KEY_VALUE_HEADS * HEAD_SIZE)
        return attend(query_rows, own_key, own_value, cached_key_rows, cached_value_rows, lengths)

    reshaped_block = (queries.reshape(N_REPLICA, LEAF_ROWS, QUERY_HEADS * HEAD_SIZE), fresh_key_rows.reshape(N_REPLICA, LEAF_ROWS, KEY_VALUE_HEADS * HEAD_SIZE),
              fresh_value_rows.reshape(N_REPLICA, LEAF_ROWS, KEY_VALUE_HEADS * HEAD_SIZE), page_numbers.reshape(N_REPLICA, LEAF_ROWS, PAGES_PER_ROW),
              context_length.reshape(N_REPLICA, LEAF_ROWS))
    attended = lax.map(attend_block, reshaped_block).reshape(LEAF_ROWS_TOTAL, QUERY_HEADS * HEAD_SIZE)
    reward = jnp.dot(attended, reward_probe, preferred_element_type=jnp.float32)
    return attended, reward
```

```python
import functools

import jax
import jax.numpy as jnp
from jax import lax
from jax.experimental import pallas as pl
from jax.experimental.pallas import tpu as pltpu
from jax.sharding import PartitionSpec as P

HEAD_SIZE = 128
TILE = 16
masked_score = -1e30
f32, bf16, i32 = jnp.float32, jnp.bfloat16, jnp.int32


def round_up(number, step):
    return -(-number // step) * step


def block_rows(capacity, heads, key_heads):
    new_rows = round_up(capacity * key_heads, TILE)
    return capacity * heads, new_rows, round_up(capacity, TILE)


def pack_kernel(capacity, q_ref, k_ref, v_ref, source_ref, parent_ref, length_ref, *rest):
    replicas = len(rest) - 6
    blocks, row_ref = rest[:replicas], rest[replicas]
    q_rows, new_rows, new_keys, new_values, taken = rest[replicas + 1 :]
    rows = q_ref.shape[0]
    heads, key_heads = q_ref.shape[1] // HEAD_SIZE, k_ref.shape[1] // HEAD_SIZE
    me = lax.axis_index("replica")
    for slot in range(replicas * capacity):
        row_ref[slot] = rows
    for replica in range(replicas):
        taken[replica] = 0
    for row in range(rows):
        source = source_ref[row]
        rank = taken[source]
        taken[source] = rank + 1
        row_ref[(source ^ me) * capacity + rank] = row
    for head in range(heads):
        lanes = slice(head * HEAD_SIZE, (head + 1) * HEAD_SIZE)
        q_rows[pl.ds(head, rows, stride=heads), :] = q_ref[:, lanes].astype(f32)
    for head in range(key_heads):
        lanes = slice(head * HEAD_SIZE, (head + 1) * HEAD_SIZE)
        new_rows[pl.ds(head, rows, stride=2 * key_heads), :] = k_ref[:, lanes].astype(f32)
        new_rows[pl.ds(key_heads + head, rows, stride=2 * key_heads), :] = v_ref[:, lanes].astype(f32)
    q_rows[rows * heads :, :] = jnp.zeros((heads, HEAD_SIZE), f32)
    new_rows[rows * 2 * key_heads :, :] = jnp.zeros((2 * key_heads, HEAD_SIZE), f32)
    q_size, new_size, meta_size = block_rows(capacity, heads, key_heads)
    if new_size != capacity * key_heads:
        new_keys[...] = jnp.zeros_like(new_keys)
        new_values[...] = jnp.zeros_like(new_values)
    at_row = lax.broadcasted_iota(i32, (meta_size, HEAD_SIZE), 0)
    at_lane = lax.broadcasted_iota(i32, (meta_size, HEAD_SIZE), 1)
    for partner, block in enumerate(blocks):
        meta = jnp.zeros((meta_size, HEAD_SIZE), f32)
        for slot in range(capacity):
            row = row_ref[partner * capacity + slot]
            block[slot * heads : (slot + 1) * heads, :] = q_rows[
                pl.ds(pl.multiple_of(row * heads, heads), heads), :
            ].astype(bf16)
            pair = new_rows[pl.ds(pl.multiple_of(row * 2 * key_heads, 2 * key_heads), 2 * key_heads), :]
            new_keys[slot * key_heads : (slot + 1) * key_heads, :] = pair[:key_heads]
            new_values[slot * key_heads : (slot + 1) * key_heads, :] = pair[key_heads:]
            real = row < rows
            held = jnp.minimum(row, rows - 1)
            parent = jnp.where(real, parent_ref[held], 0).astype(f32)
            length = jnp.where(real, length_ref[held], 0).astype(f32)
            meta = jnp.where(at_row == slot, jnp.where(at_lane == 0, parent, length), meta)
        block[q_size : q_size + new_size, :] = new_keys[...].astype(bf16)
        block[q_size + new_size : q_size + 2 * new_size, :] = new_values[...].astype(bf16)
        block[q_size + 2 * new_size :, :] = meta.astype(bf16)


def serve_kernel(capacity, heads, table_ref, block_ref, key_ref, value_ref, out_ref):
    pages_per_row = table_ref.shape[1]
    positions = key_ref.shape[1]
    key_heads = key_ref.shape[2] // HEAD_SIZE
    group = heads // key_heads
    span = pages_per_row * positions
    scaling = 1.0 / HEAD_SIZE**0.5
    q_size, new_size, meta_size = block_rows(capacity, heads, key_heads)
    meta = block_ref[q_size + 2 * new_size :, :].astype(f32)
    at_row = lax.broadcasted_iota(i32, meta.shape, 0)
    at_lane = lax.broadcasted_iota(i32, meta.shape, 1)
    rows = table_ref.shape[0]
    coded = jnp.where(at_lane == 0, meta, jnp.where(at_lane == 1, meta * rows, 0.0))
    per_tile = TILE // key_heads
    lanes = lax.broadcasted_iota(i32, (group, span + TILE), 1)
    for slot in range(capacity):
        code = jnp.sum(jnp.where(at_row == slot, coded, 0.0)).astype(i32)
        parent, length = lax.rem(code, rows), code // rows
        pages = [table_ref[parent, i] for i in range(pages_per_row)]
        tile = slot // per_tile * TILE
        own_keys = block_ref[q_size + tile : q_size + tile + TILE, :]
        own_values = block_ref[q_size + new_size + tile : q_size + new_size + tile + TILE, :]
        results = []
        q_slot = block_ref[slot * heads : (slot + 1) * heads, :]
        for head in range(key_heads):
            columns = slice(head * HEAD_SIZE, (head + 1) * HEAD_SIZE)
            keys = jnp.concatenate([key_ref[page, :, columns] for page in pages] + [own_keys], axis=0)
            values = jnp.concatenate([value_ref[page, :, columns] for page in pages] + [own_values], axis=0)
            q_group = q_slot[head * group : (head + 1) * group, :]
            scores = lax.dot_general(
                q_group, keys, (((1,), (1,)), ((), ())), preferred_element_type=f32
            )
            own = span + slot % per_tile * key_heads + head
            scores = jnp.where((lanes < length) | (lanes == own), scores * scaling, masked_score)
            peak = jnp.max(scores, axis=1, keepdims=True)
            weights = jnp.exp(scores - peak)
            denominator = jnp.sum(weights, axis=1, keepdims=True)
            numerator = jnp.dot(weights.astype(bf16), values, preferred_element_type=f32)
            results.append(numerator / denominator)
        out_ref[slot * heads : (slot + 1) * heads, :] = jnp.concatenate(results, axis=0).astype(bf16)


def unpack_kernel(capacity, heads, rows, row_ref, probe_ref, *rest):
    answers, (out_ref, reward_ref, gathered) = rest[:-3], rest[-3:]
    for partner, answer in enumerate(answers):
        for slot in range(capacity):
            row = row_ref[partner * capacity + slot]
            gathered[pl.ds(pl.multiple_of(row * heads, heads), heads), :] = answer[
                slot * heads : (slot + 1) * heads, :
            ].astype(f32)
    total = jnp.zeros((rows, HEAD_SIZE), f32)
    for head in range(heads):
        part = gathered[pl.ds(head, rows, stride=heads), :]
        out_ref[:, head * HEAD_SIZE : (head + 1) * HEAD_SIZE] = part.astype(bf16)
        total = total + part * probe_ref[:, head * HEAD_SIZE : (head + 1) * HEAD_SIZE].astype(f32)
    reward_ref[...] = jnp.sum(total.T, axis=0, keepdims=True)


def shards(
    queries,
    fresh_key_rows,
    fresh_value_rows,
    paged_key_store,
    paged_value_store,
    page_table,
    parent_replica,
    parent_slot,
    context_length,
    reward_probe,
):
    replicas = lax.axis_size("replica")
    rows = queries.shape[0]
    capacity = max(2, 2 * rows // replicas)
    heads = queries.shape[1] // HEAD_SIZE
    key_heads = fresh_key_rows.shape[1] // HEAD_SIZE
    block_size = sum(n * k for n, k in zip(block_rows(capacity, heads, key_heads), (1, 2, 1)))
    vmem, smem = pl.BlockSpec(memory_space=pltpu.VMEM), pl.BlockSpec(memory_space=pltpu.SMEM)
    params = pltpu.CompilerParams(vmem_limit_bytes=16 * 2**20)

    def in_vmem(x):
        return pltpu.with_memory_space_constraint(x, pltpu.VMEM)

    packed = pl.pallas_call(
        functools.partial(pack_kernel, capacity),
        out_shape=[pltpu.VMEM((block_size, HEAD_SIZE), bf16)] * replicas
        + [jax.ShapeDtypeStruct((replicas * capacity,), i32)],
        in_specs=[vmem] * 3 + [smem] * 3,
        out_specs=[vmem] * replicas + [smem],
        scratch_shapes=[
            pltpu.VMEM(((rows + 1) * heads, HEAD_SIZE), f32),
            pltpu.VMEM(((rows + 1) * 2 * key_heads, HEAD_SIZE), f32),
            pltpu.VMEM((block_rows(capacity, heads, key_heads)[1], HEAD_SIZE), f32),
            pltpu.VMEM((block_rows(capacity, heads, key_heads)[1], HEAD_SIZE), f32),
            pltpu.SMEM((replicas,), i32),
        ],
        compiler_params=params,
        name="pack",
    )(queries, fresh_key_rows, fresh_value_rows, parent_replica[:, 0], parent_slot[:, 0], context_length)
    blocks, slot_rows = packed[:replicas], packed[replicas]
    keys, values = in_vmem(paged_key_store), in_vmem(paged_value_store)

    serve = pl.pallas_call(
        functools.partial(serve_kernel, capacity, heads),
        out_shape=pltpu.VMEM((capacity * heads, HEAD_SIZE), bf16),
        in_specs=[smem, vmem, vmem, vmem],
        out_specs=vmem,
        compiler_params=params,
        cost_estimate=pl.CostEstimate(flops=10**7, bytes_accessed=2 * 10**6, transcendentals=0),
        name="serve",
    )

    def swap(x, partner):
        return lax.ppermute(x, "replica", [(i, i ^ partner) for i in range(replicas)])

    far_first = sorted(range(1, replicas), key=lambda m: (-m.bit_length(), m))
    answers = [None] * replicas
    arrived = {m: swap(blocks[m], m) for m in far_first}
    for m in far_first:
        answers[m] = swap(serve(page_table, in_vmem(arrived[m]), keys, values), m)
    answers[0] = serve(page_table, in_vmem(blocks[0]), keys, values)

    attended, partial_reward = pl.pallas_call(
        functools.partial(unpack_kernel, capacity, heads, rows),
        out_shape=[
            jax.ShapeDtypeStruct((rows, heads * HEAD_SIZE), bf16),
            jax.ShapeDtypeStruct((1, rows), f32),
        ],
        in_specs=[smem] + [vmem] * (replicas + 1),
        out_specs=[vmem] * 2,
        scratch_shapes=[pltpu.VMEM(((rows + 1) * heads, HEAD_SIZE), f32)],
        compiler_params=params,
        name="unpack",
    )(slot_rows, reward_probe.reshape(1, -1), *[in_vmem(x) for x in answers])
    return attended, lax.psum(partial_reward[0], "tensor")


def solution(mesh):
    placed = (
        P(("groups", "replica"), "tensor"),
        P(("groups", "replica"), "tensor"),
        P(("groups", "replica"), "tensor"),
        P(("groups", "replica"), None, "tensor"),
        P(("groups", "replica"), None, "tensor"),
        P(("groups", "replica"), None),
        P(("groups", "replica"), None),
        P(("groups", "replica"), None),
        P(("groups", "replica")),
        P("tensor"),
    )
    return jax.shard_map(
        shards,
        mesh=mesh,
        in_specs=placed,
        out_specs=(P(("groups", "replica"), "tensor"), P(("groups", "replica"))),
        check_vma=False,
    )
```

```python
import functools

import jax
import jax.numpy as jnp
from jax import lax
from jax.experimental import pallas as pl
from jax.experimental.pallas import tpu as pltpu
from jax.sharding import PartitionSpec as P

HEAD_SIZE = 128
TILE = 16
masked_score = -1e30
f32, bf16, i32 = jnp.float32, jnp.bfloat16, jnp.int32


def round_up(number, step):
    return -(-number // step) * step


def block_rows(capacity, heads, key_heads):
    new_rows = round_up(capacity * key_heads, TILE)
    return capacity * heads, new_rows, round_up(capacity, TILE)


def pack_kernel(
    capacity, q_hbm, k_hbm, v_hbm, key_hbm, value_hbm, table_hbm, source_hbm, parent_hbm, length_hbm, *rest
):
    replicas = len(rest) - 16
    blocks = rest[:replicas]
    keys_ref, values_ref, table_ref, row_ref = rest[replicas : replicas + 4]
    q_ref, k_ref, v_ref, source_ref, parent_ref, length_ref = rest[replicas + 4 : replicas + 10]
    q_rows, new_rows, new_keys, new_values, taken, arrived = rest[replicas + 10 :]
    copies = [
        pltpu.make_async_copy(source, target, arrived.at[i])
        for i, (source, target) in enumerate(
            (
                (source_hbm, source_ref),
                (q_hbm, q_ref),
                (k_hbm, k_ref),
                (v_hbm, v_ref),
                (parent_hbm, parent_ref),
                (length_hbm, length_ref),
                (table_hbm, table_ref),
                (key_hbm, keys_ref),
                (value_hbm, values_ref),
            )
        )
    ]
    for copy in copies:
        copy.start()
    rows = q_ref.shape[0]
    heads, key_heads = q_ref.shape[1] // HEAD_SIZE, k_ref.shape[1] // HEAD_SIZE
    me = lax.axis_index("replica")
    for slot in range(replicas * capacity):
        row_ref[slot] = rows
    for replica in range(replicas):
        taken[replica] = 0
    q_rows[rows * heads :, :] = jnp.zeros((heads, HEAD_SIZE), f32)
    new_rows[rows * 2 * key_heads :, :] = jnp.zeros((2 * key_heads, HEAD_SIZE), f32)
    q_size, new_size, meta_size = block_rows(capacity, heads, key_heads)
    if new_size != capacity * key_heads:
        new_keys[...] = jnp.zeros_like(new_keys)
        new_values[...] = jnp.zeros_like(new_values)
    copies[0].wait()
    for row in range(rows):
        source = source_ref[row]
        rank = taken[source]
        taken[source] = rank + 1
        row_ref[(source ^ me) * capacity + rank] = row
    for copy in copies[1:6]:
        copy.wait()
    for head in range(heads):
        lanes = slice(head * HEAD_SIZE, (head + 1) * HEAD_SIZE)
        q_rows[pl.ds(head, rows, stride=heads), :] = q_ref[:, lanes].astype(f32)
    for head in range(key_heads):
        lanes = slice(head * HEAD_SIZE, (head + 1) * HEAD_SIZE)
        new_rows[pl.ds(head, rows, stride=2 * key_heads), :] = k_ref[:, lanes].astype(f32)
        new_rows[pl.ds(key_heads + head, rows, stride=2 * key_heads), :] = v_ref[:, lanes].astype(f32)
    at_row = lax.broadcasted_iota(i32, (meta_size, HEAD_SIZE), 0)
    at_lane = lax.broadcasted_iota(i32, (meta_size, HEAD_SIZE), 1)
    for partner, block in enumerate(blocks):
        meta = jnp.zeros((meta_size, HEAD_SIZE), f32)
        for slot in range(capacity):
            row = row_ref[partner * capacity + slot]
            block[slot * heads : (slot + 1) * heads, :] = q_rows[
                pl.ds(pl.multiple_of(row * heads, heads), heads), :
            ].astype(bf16)
            pair = new_rows[pl.ds(pl.multiple_of(row * 2 * key_heads, 2 * key_heads), 2 * key_heads), :]
            new_keys[slot * key_heads : (slot + 1) * key_heads, :] = pair[:key_heads]
            new_values[slot * key_heads : (slot + 1) * key_heads, :] = pair[key_heads:]
            real = row < rows
            held = jnp.minimum(row, rows - 1)
            parent = jnp.where(real, parent_ref[held], 0).astype(f32)
            length = jnp.where(real, length_ref[held], 0).astype(f32)
            meta = jnp.where(at_row == slot, jnp.where(at_lane == 0, parent, length), meta)
        block[q_size : q_size + new_size, :] = new_keys[...].astype(bf16)
        block[q_size + new_size : q_size + 2 * new_size, :] = new_values[...].astype(bf16)
        block[q_size + 2 * new_size :, :] = meta.astype(bf16)
    for copy in copies[6:]:
        copy.wait()


def serve_kernel(capacity, heads, table_ref, block_ref, key_ref, value_ref, out_ref):
    pages_per_row, rows = table_ref.shape
    positions, width = key_ref.shape[1:]
    key_heads = width // HEAD_SIZE
    group = heads // key_heads
    span = pages_per_row * positions
    scaling = 1.0 / HEAD_SIZE**0.5
    q_size, new_size, meta_size = block_rows(capacity, heads, key_heads)
    per_tile = TILE // key_heads

    def iota(shape, axis):
        return lax.broadcasted_iota(i32, shape, axis)

    meta = block_ref[q_size + 2 * new_size :, :].astype(f32)
    at_row, at_lane = iota(meta.shape, 0), iota(meta.shape, 1)
    coded = jnp.where(at_lane == 0, meta, jnp.where(at_lane == 1, meta * rows, 0.0))
    codes = [jnp.sum(jnp.where(at_row == slot, coded, 0.0)) for slot in range(capacity)]
    codes = [code.astype(i32) for code in codes]
    lengths = [code // rows for code in codes]
    parents = [code - length * rows for code, length in zip(codes, lengths)]
    pages = [[table_ref[i, parent] for i in range(pages_per_row)] for parent in parents]
    diagonal = iota((heads, width), 0) // group == iota((heads, width), 1) // HEAD_SIZE
    own_lane = iota((heads, TILE), 1) - iota((heads, TILE), 0) // group
    seen = iota((heads, span), 1)
    scores, own_scores = [], []
    for slot in range(capacity):
        tile = slot // per_tile * TILE
        own_keys = block_ref[q_size + tile : q_size + tile + TILE, :]
        q_slot = block_ref[slot * heads : (slot + 1) * heads, :]
        keys = jnp.concatenate([key_ref[page] for page in pages[slot]], axis=0)
        spread = jnp.where(diagonal, jnp.concatenate([q_slot] * key_heads, axis=1), jnp.zeros((), bf16))
        by_lanes = (((1,), (1,)), ((), ()))
        scores.append(lax.dot_general(spread, keys, by_lanes, preferred_element_type=f32))
        own_scores.append(lax.dot_general(q_slot, own_keys, by_lanes, preferred_element_type=f32))
    weights, own_weights, denominators = [], [], []
    for slot in range(capacity):
        included = jnp.where(seen < lengths[slot], scores[slot] * scaling, masked_score)
        own = jnp.where(own_lane == slot % per_tile * key_heads, own_scores[slot] * scaling, masked_score)
        peak = jnp.maximum(jnp.max(included, axis=1, keepdims=True), jnp.max(own, axis=1, keepdims=True))
        weight, own_weight = jnp.exp(included - peak), jnp.exp(own - peak)
        denominators.append(
            jnp.sum(weight, axis=1, keepdims=True) + jnp.sum(own_weight, axis=1, keepdims=True)
        )
        weights.append(weight.astype(bf16))
        own_weights.append(own_weight.astype(bf16))
    for slot in range(capacity):
        tile = slot // per_tile * TILE
        own_values = block_ref[q_size + new_size + tile : q_size + new_size + tile + TILE, :]
        values = jnp.concatenate([value_ref[page] for page in pages[slot]], axis=0)
        wide = jnp.dot(weights[slot], values, preferred_element_type=f32)
        numerator = jnp.concatenate(
            [
                wide[head * group : (head + 1) * group, head * HEAD_SIZE : (head + 1) * HEAD_SIZE]
                for head in range(key_heads)
            ],
            axis=0,
        ) + jnp.dot(own_weights[slot], own_values, preferred_element_type=f32)
        out_ref[slot * heads : (slot + 1) * heads, :] = (numerator / denominators[slot]).astype(bf16)


def unpack_kernel(capacity, heads, rows, row_ref, probe_ref, *rest):
    answers, (out_ref, reward_ref, gathered) = rest[:-3], rest[-3:]
    for partner, answer in enumerate(answers):
        for slot in range(capacity):
            row = row_ref[partner * capacity + slot]
            gathered[pl.ds(pl.multiple_of(row * heads, heads), heads), :] = answer[
                slot * heads : (slot + 1) * heads, :
            ].astype(f32)
    total = jnp.zeros((rows, HEAD_SIZE), f32)
    for head in range(heads):
        part = gathered[pl.ds(head, rows, stride=heads), :]
        out_ref[:, head * HEAD_SIZE : (head + 1) * HEAD_SIZE] = part.astype(bf16)
        total = total + part * probe_ref[:, head * HEAD_SIZE : (head + 1) * HEAD_SIZE].astype(f32)
    reward_ref[...] = jnp.sum(total.T, axis=0, keepdims=True)


def shards(
    queries,
    fresh_key_rows,
    fresh_value_rows,
    paged_key_store,
    paged_value_store,
    page_table,
    parent_replica,
    parent_slot,
    context_length,
    reward_probe,
):
    replicas = lax.axis_size("replica")
    rows = queries.shape[0]
    capacity = max(2, 2 * rows // replicas)
    heads = queries.shape[1] // HEAD_SIZE
    key_heads = fresh_key_rows.shape[1] // HEAD_SIZE
    q_size, new_size, meta_size = block_rows(capacity, heads, key_heads)
    block_size = q_size + 2 * new_size + meta_size
    vmem, smem = pl.BlockSpec(memory_space=pltpu.VMEM), pl.BlockSpec(memory_space=pltpu.SMEM)
    params = pltpu.CompilerParams(vmem_limit_bytes=16 * 2**20)

    def in_vmem(x):
        return pltpu.with_memory_space_constraint(x, pltpu.VMEM)

    def in_smem(x):
        return pltpu.with_memory_space_constraint(x, pltpu.SMEM)

    given = (
        queries,
        fresh_key_rows,
        fresh_value_rows,
        paged_key_store,
        paged_value_store,
        page_table.T,
        parent_replica[:, 0],
        parent_slot[:, 0],
        context_length,
    )
    packed = pl.pallas_call(
        functools.partial(pack_kernel, capacity),
        out_shape=[pltpu.VMEM((block_size, HEAD_SIZE), bf16)] * replicas
        + [
            pltpu.VMEM(paged_key_store.shape, bf16),
            pltpu.VMEM(paged_value_store.shape, bf16),
            pltpu.SMEM(page_table.shape[::-1], i32),
            pltpu.SMEM((replicas * capacity,), i32),
        ],
        in_specs=[pl.BlockSpec(memory_space=pltpu.HBM)] * len(given),
        out_specs=[vmem] * (replicas + 2) + [smem] * 2,
        scratch_shapes=[
            pltpu.VMEM(queries.shape, bf16),
            pltpu.VMEM(fresh_key_rows.shape, bf16),
            pltpu.VMEM(fresh_value_rows.shape, bf16),
            pltpu.SMEM((rows,), i32),
            pltpu.SMEM((rows,), i32),
            pltpu.SMEM((rows,), i32),
            pltpu.VMEM(((rows + 1) * heads, HEAD_SIZE), f32),
            pltpu.VMEM(((rows + 1) * 2 * key_heads, HEAD_SIZE), f32),
            pltpu.VMEM((new_size, HEAD_SIZE), f32),
            pltpu.VMEM((new_size, HEAD_SIZE), f32),
            pltpu.SMEM((replicas,), i32),
            pltpu.SemaphoreType.DMA((len(given),)),
        ],
        compiler_params=params,
        name="pack",
    )(*[pltpu.with_memory_space_constraint(x, pltpu.HBM) for x in given])
    blocks = packed[:replicas]
    keys, values = map(in_vmem, packed[replicas : replicas + 2])
    table, slot_rows = map(in_smem, packed[replicas + 2 :])

    serve = pl.pallas_call(
        functools.partial(serve_kernel, capacity, heads),
        out_shape=pltpu.VMEM((capacity * heads, HEAD_SIZE), bf16),
        in_specs=[smem, vmem, vmem, vmem],
        out_specs=vmem,
        compiler_params=params,
        cost_estimate=pl.CostEstimate(flops=10**7, bytes_accessed=2 * 10**6, transcendentals=0),
        name="serve",
    )

    def swap(x, partner):
        return lax.ppermute(x, "replica", [(i, i ^ partner) for i in range(replicas)])

    far_first = sorted(range(1, replicas), key=lambda m: (-m.bit_length(), m))
    answers = [None] * replicas
    arrived = {m: swap(blocks[m], m) for m in far_first}
    for m in far_first:
        answers[m] = swap(serve(table, in_vmem(arrived[m]), keys, values), m)
    answers[0] = serve(table, in_vmem(blocks[0]), keys, values)

    attended, partial_reward = pl.pallas_call(
        functools.partial(unpack_kernel, capacity, heads, rows),
        out_shape=[pltpu.VMEM((rows, heads * HEAD_SIZE), bf16), pltpu.VMEM((1, rows), f32)],
        in_specs=[smem] + [vmem] * (replicas + 1),
        out_specs=[vmem] * 2,
        scratch_shapes=[pltpu.VMEM(((rows + 1) * heads, HEAD_SIZE), f32)],
        compiler_params=params,
        name="unpack",
    )(slot_rows, in_vmem(reward_probe.reshape(1, -1)), *[in_vmem(x) for x in answers])
    other_half = lax.ppermute(partial_reward, "tensor", [(0, 1), (1, 0)])
    return attended, (partial_reward + other_half)[0]


def solution(mesh):
    placed = (
        P(("groups", "replica"), "tensor"),
        P(("groups", "replica"), "tensor"),
        P(("groups", "replica"), "tensor"),
        P(("groups", "replica"), None, "tensor"),
        P(("groups", "replica"), None, "tensor"),
        P(("groups", "replica"), None),
        P(("groups", "replica"), None),
        P(("groups", "replica"), None),
        P(("groups", "replica")),
        P("tensor"),
    )
    return jax.shard_map(
        shards,
        mesh=mesh,
        in_specs=placed,
        out_specs=(P(("groups", "replica"), "tensor"), P(("groups", "replica"))),
        check_vma=False,
    )
```

```python
import functools

import jax
import jax.numpy as jnp
from jax import lax
from jax.experimental import pallas as pl
from jax.experimental.pallas import tpu as pltpu
from jax.sharding import PartitionSpec as P

HEAD_SIZE = 128
TILE = 16
TOGETHER = 2
masked_score = -1e30
f32, bf16, i32 = jnp.float32, jnp.bfloat16, jnp.int32


def round_up(number, step):
    return -(-number // step) * step


def block_rows(capacity, heads, key_heads):
    new_rows = round_up(capacity * key_heads, TILE)
    return capacity * heads, new_rows, round_up(capacity, TILE)


def partners_in_turn(replicas):
    near, far = list(range(1, replicas // 2)), list(range(replicas // 2, replicas))
    pairs = list(zip(far, near))
    even = [m for pair in pairs for m in pair] + far[len(near) :] + [0]
    odd = [m for pair in pairs for m in pair[::-1]] + far[len(near) :] + [0]
    return even, odd


def pack_kernel(
    capacity, turns, q_hbm, k_hbm, v_hbm, key_hbm, value_hbm, table_hbm, source_hbm, parent_hbm, length_hbm, *rest
):
    replicas = len(rest) - 17
    blocks = rest[:replicas]
    keys_ref, values_ref, table_ref, row_ref = rest[replicas : replicas + 4]
    q_ref, k_ref, v_ref, source_ref, parent_ref, length_ref = rest[replicas + 4 : replicas + 10]
    q_rows, new_rows, new_keys, new_values, taken, turn_ref, arrived = rest[replicas + 10 :]
    copies = [
        pltpu.make_async_copy(source, target, arrived.at[i])
        for i, (source, target) in enumerate(
            (
                (source_hbm, source_ref),
                (q_hbm, q_ref),
                (k_hbm, k_ref),
                (v_hbm, v_ref),
                (parent_hbm, parent_ref),
                (length_hbm, length_ref),
                (table_hbm, table_ref),
                (key_hbm, keys_ref),
                (value_hbm, values_ref),
            )
        )
    ]
    for copy in copies:
        copy.start()
    rows = q_ref.shape[0]
    heads, key_heads = q_ref.shape[1] // HEAD_SIZE, k_ref.shape[1] // HEAD_SIZE
    me = lax.axis_index("replica")
    for slot in range(replicas * capacity):
        row_ref[slot] = rows
    odd = lax.rem(lax.axis_index("tensor"), 2)
    for replica in range(replicas):
        taken[replica] = 0
        even_turn, odd_turn = (turn.index(replica) for turn in turns)
        turn_ref[replica] = jnp.where(odd == 1, odd_turn, even_turn)
    q_rows[rows * heads :, :] = jnp.zeros((heads, HEAD_SIZE), f32)
    new_rows[rows * 2 * key_heads :, :] = jnp.zeros((2 * key_heads, HEAD_SIZE), f32)
    q_size, new_size, meta_size = block_rows(capacity, heads, key_heads)
    if new_size != capacity * key_heads:
        new_keys[...] = jnp.zeros_like(new_keys)
        new_values[...] = jnp.zeros_like(new_values)
    copies[0].wait()
    for row in range(rows):
        source = source_ref[row]
        rank = taken[source]
        taken[source] = rank + 1
        row_ref[turn_ref[source ^ me] * capacity + rank] = row
    for copy in copies[1:6]:
        copy.wait()
    for head in range(heads):
        lanes = slice(head * HEAD_SIZE, (head + 1) * HEAD_SIZE)
        q_rows[pl.ds(head, rows, stride=heads), :] = q_ref[:, lanes].astype(f32)
    for head in range(key_heads):
        lanes = slice(head * HEAD_SIZE, (head + 1) * HEAD_SIZE)
        new_rows[pl.ds(head, rows, stride=2 * key_heads), :] = k_ref[:, lanes].astype(f32)
        new_rows[pl.ds(key_heads + head, rows, stride=2 * key_heads), :] = v_ref[:, lanes].astype(f32)
    at_row = lax.broadcasted_iota(i32, (meta_size, HEAD_SIZE), 0)
    at_lane = lax.broadcasted_iota(i32, (meta_size, HEAD_SIZE), 1)
    for partner, block in enumerate(blocks):
        meta = jnp.zeros((meta_size, HEAD_SIZE), f32)
        for slot in range(capacity):
            row = row_ref[partner * capacity + slot]
            block[slot * heads : (slot + 1) * heads, :] = q_rows[
                pl.ds(pl.multiple_of(row * heads, heads), heads), :
            ].astype(bf16)
            pair = new_rows[pl.ds(pl.multiple_of(row * 2 * key_heads, 2 * key_heads), 2 * key_heads), :]
            new_keys[slot * key_heads : (slot + 1) * key_heads, :] = pair[:key_heads]
            new_values[slot * key_heads : (slot + 1) * key_heads, :] = pair[key_heads:]
            real = row < rows
            held = jnp.minimum(row, rows - 1)
            parent = jnp.where(real, parent_ref[held], 0).astype(f32)
            length = jnp.where(real, length_ref[held], 0).astype(f32)
            meta = jnp.where(at_row == slot, jnp.where(at_lane == 0, parent, length), meta)
        block[q_size : q_size + new_size, :] = new_keys[...].astype(bf16)
        block[q_size + new_size : q_size + 2 * new_size, :] = new_values[...].astype(bf16)
        block[q_size + 2 * new_size :, :] = meta.astype(bf16)
    for copy in copies[6:]:
        copy.wait()


def serve_kernel(capacity, heads, table_ref, key_ref, value_ref, *blocks_and_answers):
    number = len(blocks_and_answers) // 2
    blocks, answers = blocks_and_answers[:number], blocks_and_answers[number:]
    pages_per_row, rows = table_ref.shape
    positions, width = key_ref.shape[1:]
    key_heads = width // HEAD_SIZE
    group = heads // key_heads
    span = pages_per_row * positions
    scaling = 1.0 / HEAD_SIZE**0.5
    q_size, new_size, meta_size = block_rows(capacity, heads, key_heads)
    per_tile = TILE // key_heads
    slots = [(n, slot) for n in range(number) for slot in range(capacity)]

    def iota(shape, axis):
        return lax.broadcasted_iota(i32, shape, axis)

    at_row, at_lane = iota((meta_size, HEAD_SIZE), 0), iota((meta_size, HEAD_SIZE), 1)
    metas = [block[q_size + 2 * new_size :, :].astype(f32) for block in blocks]
    coded = [jnp.where(at_lane == 0, meta, jnp.where(at_lane == 1, meta * rows, 0.0)) for meta in metas]
    codes = [jnp.sum(jnp.where(at_row == slot, coded[n], 0.0)).astype(i32) for n, slot in slots]
    lengths = [code // rows for code in codes]
    parents = [code - length * rows for code, length in zip(codes, lengths)]
    pages = [[table_ref[i, parent] for i in range(pages_per_row)] for parent in parents]
    diagonal = iota((heads, width), 0) // group == iota((heads, width), 1) // HEAD_SIZE
    own_lane = iota((heads, TILE), 1) - iota((heads, TILE), 0) // group
    seen = iota((heads, span), 1)
    by_lanes = (((1,), (1,)), ((), ()))
    scores, own_scores = [], []
    for (n, slot), found in zip(slots, pages):
        tile = q_size + slot // per_tile * TILE
        own_keys = blocks[n][tile : tile + TILE, :]
        q_slot = blocks[n][slot * heads : (slot + 1) * heads, :]
        keys = jnp.concatenate([key_ref[page] for page in found], axis=0)
        spread = jnp.where(diagonal, jnp.concatenate([q_slot] * key_heads, axis=1), jnp.zeros((), bf16))
        scores.append(lax.dot_general(spread, keys, by_lanes, preferred_element_type=f32))
        own_scores.append(lax.dot_general(q_slot, own_keys, by_lanes, preferred_element_type=f32))
    weights, own_weights, denominators = [], [], []
    for (_, slot), length, score, own_score in zip(slots, lengths, scores, own_scores):
        included = jnp.where(seen < length, score * scaling, masked_score)
        own = jnp.where(own_lane == slot % per_tile * key_heads, own_score * scaling, masked_score)
        peak = jnp.maximum(jnp.max(included, axis=1, keepdims=True), jnp.max(own, axis=1, keepdims=True))
        weight, own_weight = jnp.exp(included - peak), jnp.exp(own - peak)
        denominators.append(
            jnp.sum(weight, axis=1, keepdims=True) + jnp.sum(own_weight, axis=1, keepdims=True)
        )
        weights.append(weight.astype(bf16))
        own_weights.append(own_weight.astype(bf16))
    for i, (n, slot) in enumerate(slots):
        tile = q_size + new_size + slot // per_tile * TILE
        own_values = blocks[n][tile : tile + TILE, :]
        values = jnp.concatenate([value_ref[page] for page in pages[i]], axis=0)
        wide = jnp.dot(weights[i], values, preferred_element_type=f32)
        numerator = jnp.concatenate(
            [
                wide[head * group : (head + 1) * group, head * HEAD_SIZE : (head + 1) * HEAD_SIZE]
                for head in range(key_heads)
            ],
            axis=0,
        ) + jnp.dot(own_weights[i], own_values, preferred_element_type=f32)
        answers[n][slot * heads : (slot + 1) * heads, :] = (numerator / denominators[i]).astype(bf16)


def unpack_kernel(capacity, heads, rows, row_ref, probe_ref, *rest):
    answers, (out_ref, reward_ref, gathered) = rest[:-3], rest[-3:]
    for partner, answer in enumerate(answers):
        for slot in range(capacity):
            row = row_ref[partner * capacity + slot]
            gathered[pl.ds(pl.multiple_of(row * heads, heads), heads), :] = answer[
                slot * heads : (slot + 1) * heads, :
            ].astype(f32)
    total = jnp.zeros((rows, HEAD_SIZE), f32)
    for head in range(heads):
        part = gathered[pl.ds(head, rows, stride=heads), :]
        out_ref[:, head * HEAD_SIZE : (head + 1) * HEAD_SIZE] = part.astype(bf16)
        total = total + part * probe_ref[:, head * HEAD_SIZE : (head + 1) * HEAD_SIZE].astype(f32)
    reward_ref[...] = jnp.sum(total.T, axis=0, keepdims=True)


def shards(
    queries,
    fresh_key_rows,
    fresh_value_rows,
    paged_key_store,
    paged_value_store,
    page_table,
    parent_replica,
    parent_slot,
    context_length,
    reward_probe,
):
    replicas = lax.axis_size("replica")
    rows = queries.shape[0]
    capacity = max(2, 2 * rows // replicas)
    heads = queries.shape[1] // HEAD_SIZE
    key_heads = fresh_key_rows.shape[1] // HEAD_SIZE
    q_size, new_size, meta_size = block_rows(capacity, heads, key_heads)
    block_size = q_size + 2 * new_size + meta_size
    vmem, smem = pl.BlockSpec(memory_space=pltpu.VMEM), pl.BlockSpec(memory_space=pltpu.SMEM)
    params = pltpu.CompilerParams(vmem_limit_bytes=16 * 2**20)

    def in_vmem(x):
        return pltpu.with_memory_space_constraint(x, pltpu.VMEM)

    def in_smem(x):
        return pltpu.with_memory_space_constraint(x, pltpu.SMEM)

    turns = partners_in_turn(replicas)
    given = (
        queries,
        fresh_key_rows,
        fresh_value_rows,
        paged_key_store,
        paged_value_store,
        page_table.T,
        parent_replica[:, 0],
        parent_slot[:, 0],
        context_length,
    )
    packed = pl.pallas_call(
        functools.partial(pack_kernel, capacity, turns),
        out_shape=[pltpu.VMEM((block_size, HEAD_SIZE), bf16)] * replicas
        + [
            pltpu.VMEM(paged_key_store.shape, bf16),
            pltpu.VMEM(paged_value_store.shape, bf16),
            pltpu.SMEM(page_table.shape[::-1], i32),
            pltpu.SMEM((replicas * capacity,), i32),
        ],
        in_specs=[pl.BlockSpec(memory_space=pltpu.HBM)] * len(given),
        out_specs=[vmem] * (replicas + 2) + [smem] * 2,
        scratch_shapes=[
            pltpu.VMEM(queries.shape, bf16),
            pltpu.VMEM(fresh_key_rows.shape, bf16),
            pltpu.VMEM(fresh_value_rows.shape, bf16),
            pltpu.SMEM((rows,), i32),
            pltpu.SMEM((rows,), i32),
            pltpu.SMEM((rows,), i32),
            pltpu.VMEM(((rows + 1) * heads, HEAD_SIZE), f32),
            pltpu.VMEM(((rows + 1) * 2 * key_heads, HEAD_SIZE), f32),
            pltpu.VMEM((new_size, HEAD_SIZE), f32),
            pltpu.VMEM((new_size, HEAD_SIZE), f32),
            pltpu.SMEM((replicas,), i32),
            pltpu.SMEM((replicas,), i32),
            pltpu.SemaphoreType.DMA((len(given),)),
        ],
        compiler_params=params,
        name="pack",
    )(*[pltpu.with_memory_space_constraint(x, pltpu.HBM) for x in given])
    blocks = packed[:replicas]
    keys, values = map(in_vmem, packed[replicas : replicas + 2])
    table, slot_rows = map(in_smem, packed[replicas + 2 :])

    def serve(asked):
        return pl.pallas_call(
            functools.partial(serve_kernel, capacity, heads),
            out_shape=[pltpu.VMEM((capacity * heads, HEAD_SIZE), bf16)] * len(asked),
            in_specs=[smem] + [vmem] * (2 + len(asked)),
            out_specs=[vmem] * len(asked),
            compiler_params=params,
            cost_estimate=pl.CostEstimate(flops=10**7, bytes_accessed=2 * 10**6, transcendentals=0),
            name="serve",
        )(table, keys, values, *map(in_vmem, asked))

    def swap(x, turn):
        cores = lax.axis_size("tensor")
        pairs = [
            (i * cores + core, (i ^ turns[core % 2][turn]) * cores + core)
            for i in range(replicas)
            for core in range(cores)
        ]
        return lax.ppermute(x, ("replica", "tensor"), pairs)

    arrived = [swap(blocks[turn], turn) for turn in range(replicas - 1)] + [blocks[-1]]
    answers = []
    for turn in range(0, replicas, TOGETHER):
        for answer in serve(arrived[turn : turn + TOGETHER]):
            answers.append(swap(answer, len(answers)) if len(answers) < replicas - 1 else answer)

    attended, partial_reward = pl.pallas_call(
        functools.partial(unpack_kernel, capacity, heads, rows),
        out_shape=[pltpu.VMEM((rows, heads * HEAD_SIZE), bf16), pltpu.VMEM((1, rows), f32)],
        in_specs=[smem] + [vmem] * (replicas + 1),
        out_specs=[vmem] * 2,
        scratch_shapes=[pltpu.VMEM(((rows + 1) * heads, HEAD_SIZE), f32)],
        compiler_params=params,
        name="unpack",
    )(slot_rows, in_vmem(reward_probe.reshape(1, -1)), *[in_vmem(x) for x in answers])
    other_half = lax.ppermute(partial_reward, "tensor", [(0, 1), (1, 0)])
    return attended, (partial_reward + other_half)[0]


def solution(mesh):
    placed = (
        P(("groups", "replica"), "tensor"),
        P(("groups", "replica"), "tensor"),
        P(("groups", "replica"), "tensor"),
        P(("groups", "replica"), None, "tensor"),
        P(("groups", "replica"), None, "tensor"),
        P(("groups", "replica"), None),
        P(("groups", "replica"), None),
        P(("groups", "replica"), None),
        P(("groups", "replica")),
        P("tensor"),
    )
    return jax.shard_map(
        shards,
        mesh=mesh,
        in_specs=placed,
        out_specs=(P(("groups", "replica"), "tensor"), P(("groups", "replica"))),
        check_vma=False,
    )
```

```python
import functools

import jax
import jax.numpy as jnp
from jax import lax
from jax.experimental import pallas as pl
from jax.experimental.pallas import tpu as pltpu
from jax.sharding import PartitionSpec as P

HEAD_SIZE = 128
TILE = 16
TOGETHER = 2
masked_score = -1e30
f32, bf16, i32 = jnp.float32, jnp.bfloat16, jnp.int32


def round_up(number, step):
    return -(-number // step) * step


def block_rows(capacity, heads, key_heads):
    return capacity * heads, round_up(capacity * key_heads, TILE), round_up(capacity, TILE)


def iota(shape, axis):
    return lax.broadcasted_iota(i32, shape, axis)


def partners_in_turn(replicas):
    near, far = list(range(1, replicas // 2)), list(range(replicas // 2, replicas))
    pairs = list(zip(far, near))
    even = [m for pair in pairs for m in pair] + far[len(near) :] + [0]
    odd = [m for pair in pairs for m in pair[::-1]] + far[len(near) :] + [0]
    return even, odd


def start_copies(sources, targets, arrived):
    copies = [
        pltpu.make_async_copy(source, target, arrived.at[i])
        for i, (source, target) in enumerate(zip(sources, targets))
    ]
    for copy in copies:
        copy.start()
    return copies


def fill(blocks, capacity, heads, key_heads, row_ref, q_rows, value_rows, facts, new_values, meta):
    q_size, new_size, _ = block_rows(capacity, heads, key_heads)
    step = round_up(key_heads, 8)
    for turn, block in enumerate(blocks):
        for slot in range(capacity):
            row = row_ref[turn * capacity + slot]
            block[slot * heads : (slot + 1) * heads, :] = q_rows[
                pl.ds(pl.multiple_of(row * heads, heads), heads), :
            ].astype(bf16)
            own = value_rows[pl.ds(pl.multiple_of(row * step, step), step), :]
            new_values[slot * key_heads : (slot + 1) * key_heads, :] = own[:key_heads]
            meta[slot : slot + 1, :] = facts[pl.ds(row, 1), :]
        block[q_size : q_size + new_size, :] = new_values[...].astype(bf16)
        block[q_size + new_size :, :] = meta[...].astype(bf16)


def pack_kernel(
    capacity,
    turns,
    q_hbm,
    k_hbm,
    v_hbm,
    source_hbm,
    parent_hbm,
    length_hbm,
    table_hbm,
    key_hbm,
    value_hbm,
    *rest,
):
    replicas = len(turns[0])
    blocks, rest = rest[:replicas], rest[replicas:]
    row_ref, table_ref, keys_ref, values_ref = rest[:4]
    q_ref, k_ref, v_ref, source_ref, parent_ref, length_ref = rest[4:10]
    q_rows, value_rows, facts, new_values, meta, taken, turn_ref, arrived = rest[10:]
    copies = start_copies(
        (source_hbm, q_hbm, k_hbm, v_hbm, parent_hbm, length_hbm, table_hbm, key_hbm, value_hbm),
        (source_ref, q_ref, k_ref, v_ref, parent_ref, length_ref, table_ref, keys_ref, values_ref),
        arrived,
    )
    rows = q_ref.shape[0]
    heads, key_heads = q_ref.shape[1] // HEAD_SIZE, k_ref.shape[1] // HEAD_SIZE
    step = round_up(key_heads, 8)
    me, odd = lax.axis_index("replica"), lax.rem(lax.axis_index("tensor"), 2)
    for slot in range(replicas * capacity):
        row_ref[slot] = rows
    for replica in range(replicas):
        taken[replica] = 0
        even_turn, odd_turn = (turn.index(replica) for turn in turns)
        turn_ref[replica] = jnp.where(odd == 1, odd_turn, even_turn)
    q_rows[rows * heads :, :] = jnp.zeros((heads, HEAD_SIZE), f32)
    value_rows[rows * step :, :] = jnp.zeros((step, HEAD_SIZE), f32)
    facts[rows:, :] = jnp.zeros((facts.shape[0] - rows, HEAD_SIZE), f32)
    new_values[...] = jnp.zeros_like(new_values)
    meta[...] = jnp.zeros_like(meta)
    copies[0].wait()
    for row in range(rows):
        source = source_ref[row]
        rank = taken[source]
        taken[source] = rank + 1
        row_ref[turn_ref[source ^ me] * capacity + rank] = row
    for copy in copies[1:6]:
        copy.wait()
    lane = iota((rows, HEAD_SIZE), 1)
    own = jnp.zeros((rows, HEAD_SIZE), f32)
    for head in range(heads):
        lanes = slice(head * HEAD_SIZE, (head + 1) * HEAD_SIZE)
        q_head = q_ref[:, lanes].astype(f32)
        q_rows[pl.ds(head, rows, stride=heads), :] = q_head
        key_head = head // (heads // key_heads)
        if head % (heads // key_heads) == 0:
            lanes = slice(key_head * HEAD_SIZE, (key_head + 1) * HEAD_SIZE)
            k_head = k_ref[:, lanes].astype(f32)
            value_rows[pl.ds(key_head, rows, stride=step), :] = v_ref[:, lanes].astype(f32)
        score = jnp.sum(q_head * k_head, axis=1, keepdims=True)
        own = jnp.where(lane % heads == head, score, own)
    high = own.astype(bf16).astype(f32)
    middle = (own - high).astype(bf16).astype(f32)
    low = own - high - middle
    part = lane // heads
    own = jnp.where(part == 1, high, jnp.where(part == 2, middle, jnp.where(part == 3, low, 0.0)))
    diagonal = iota((rows, rows), 0) == iota((rows, rows), 1)

    def column(ref):
        return jnp.sum(jnp.where(diagonal, ref[...].astype(f32), 0.0), axis=1, keepdims=True)

    facts[:rows, :] = jnp.where(lane == 0, column(parent_ref), jnp.where(lane == 1, column(length_ref), own))
    fill(blocks, capacity, heads, key_heads, row_ref, q_rows, value_rows, facts, new_values, meta)
    for copy in copies[6:]:
        copy.wait()


def serve_kernel(capacity, heads, table_ref, key_ref, value_ref, *blocks_and_answers):
    number = len(blocks_and_answers) // 2
    blocks, answers = blocks_and_answers[:number], blocks_and_answers[number:]
    pages_per_row, rows = table_ref.shape
    positions, width = key_ref.shape[1:]
    key_heads = width // HEAD_SIZE
    group = heads // key_heads
    span = pages_per_row * positions
    scaling = 1.0 / HEAD_SIZE**0.5
    q_size, new_size, meta_size = block_rows(capacity, heads, key_heads)
    per_tile = TILE // key_heads
    slots = [(n, slot) for n in range(number) for slot in range(capacity)]

    at_row, at_lane = iota((meta_size, HEAD_SIZE), 0), iota((meta_size, HEAD_SIZE), 1)
    metas = [block[q_size + new_size :, :].astype(f32) for block in blocks]
    at_lane_of_head = iota((heads, HEAD_SIZE), 1)
    picked = (at_lane_of_head % heads == iota((heads, HEAD_SIZE), 0)) & (at_lane_of_head >= heads)
    by_lanes = (((1,), (1,)), ((), ()))
    picked = jnp.where(picked, 1.0, 0.0).astype(bf16)
    coded = [jnp.where(at_lane == 0, meta, jnp.where(at_lane == 1, meta * rows, 0.0)) for meta in metas]
    codes = [jnp.sum(jnp.where(at_row == slot, coded[n], 0.0)).astype(i32) for n, slot in slots]
    lengths = [code // rows for code in codes]
    parents = [code - length * rows for code, length in zip(codes, lengths)]
    pages = [[table_ref[i, parent] for i in range(pages_per_row)] for parent in parents]
    diagonal = iota((heads, width), 0) // group == iota((heads, width), 1) // HEAD_SIZE
    own_lane = iota((heads, TILE), 1) - iota((heads, TILE), 0) // group
    seen = iota((heads, span), 1)
    scores, new_scores = [], []
    for (n, slot), found in zip(slots, pages):
        q_slot = blocks[n][slot * heads : (slot + 1) * heads, :]
        keys = jnp.concatenate([key_ref[page] for page in found], axis=0)
        spread = jnp.where(diagonal, jnp.concatenate([q_slot] * key_heads, axis=1), jnp.zeros((), bf16))
        scores.append(lax.dot_general(spread, keys, by_lanes, preferred_element_type=f32))
        parts = jnp.broadcast_to(metas[n][slot : slot + 1, :], (TILE, HEAD_SIZE)).astype(bf16)
        new_scores.append(lax.dot_general(picked, parts, by_lanes, preferred_element_type=f32))
    weights, own_weights, denominators = [], [], []
    for (_, slot), length, score, new_score in zip(slots, lengths, scores, new_scores):
        included = jnp.where(seen < length, score * scaling, masked_score)
        own = jnp.where(own_lane == slot % per_tile * key_heads, new_score * scaling, masked_score)
        peak = jnp.maximum(jnp.max(included, axis=1, keepdims=True), jnp.max(own, axis=1, keepdims=True))
        weight, own_weight = jnp.exp(included - peak), jnp.exp(own - peak)
        denominators.append(
            jnp.sum(weight, axis=1, keepdims=True) + jnp.sum(own_weight, axis=1, keepdims=True)
        )
        weights.append(weight.astype(bf16))
        own_weights.append(own_weight.astype(bf16))
    for i, (n, slot) in enumerate(slots):
        tile = q_size + slot // per_tile * TILE
        own_values = blocks[n][tile : tile + TILE, :]
        values = jnp.concatenate([value_ref[page] for page in pages[i]], axis=0)
        wide = jnp.dot(weights[i], values, preferred_element_type=f32)
        numerator = jnp.concatenate(
            [
                wide[head * group : (head + 1) * group, head * HEAD_SIZE : (head + 1) * HEAD_SIZE]
                for head in range(key_heads)
            ],
            axis=0,
        ) + jnp.dot(own_weights[i], own_values, preferred_element_type=f32)
        answers[n][slot * heads : (slot + 1) * heads, :] = (numerator / denominators[i]).astype(bf16)


def unpack_kernel(capacity, heads, rows, row_ref, probe_ref, *rest):
    answers, (out_ref, reward_ref, gathered) = rest[:-3], rest[-3:]
    for partner, answer in enumerate(answers):
        for slot in range(capacity):
            row = row_ref[partner * capacity + slot]
            gathered[pl.ds(pl.multiple_of(row * heads, heads), heads), :] = answer[
                slot * heads : (slot + 1) * heads, :
            ].astype(f32)
    total = jnp.zeros((rows, HEAD_SIZE), f32)
    for head in range(heads):
        part = gathered[pl.ds(head, rows, stride=heads), :]
        out_ref[:, head * HEAD_SIZE : (head + 1) * HEAD_SIZE] = part.astype(bf16)
        total = total + part * probe_ref[:, head * HEAD_SIZE : (head + 1) * HEAD_SIZE].astype(f32)
    reward_ref[...] = jnp.sum(total.T, axis=0, keepdims=True)


def shards(
    queries,
    fresh_key_rows,
    fresh_value_rows,
    paged_key_store,
    paged_value_store,
    page_table,
    parent_replica,
    parent_slot,
    context_length,
    reward_probe,
):
    replicas = lax.axis_size("replica")
    rows = queries.shape[0]
    capacity = max(2, 2 * rows // replicas)
    heads = queries.shape[1] // HEAD_SIZE
    key_heads = fresh_key_rows.shape[1] // HEAD_SIZE
    q_size, new_size, meta_size = block_rows(capacity, heads, key_heads)
    block_size = q_size + new_size + meta_size
    step = round_up(key_heads, 8)
    vmem, smem = pl.BlockSpec(memory_space=pltpu.VMEM), pl.BlockSpec(memory_space=pltpu.SMEM)
    params = pltpu.CompilerParams(vmem_limit_bytes=16 * 2**20)

    def in_vmem(x):
        return pltpu.with_memory_space_constraint(x, pltpu.VMEM)

    def in_smem(x):
        return pltpu.with_memory_space_constraint(x, pltpu.SMEM)

    turns = partners_in_turn(replicas)
    given = (
        queries,
        fresh_key_rows,
        fresh_value_rows,
        parent_replica[:, 0],
        parent_slot.reshape(1, rows),
        context_length.reshape(1, rows),
        page_table.T,
        paged_key_store,
        paged_value_store,
    )
    packed = pl.pallas_call(
        functools.partial(pack_kernel, capacity, turns),
        out_shape=[pltpu.VMEM((block_size, HEAD_SIZE), bf16)] * replicas
        + [
            pltpu.SMEM((replicas * capacity,), i32),
            pltpu.SMEM(page_table.shape[::-1], i32),
            pltpu.VMEM(paged_key_store.shape, bf16),
            pltpu.VMEM(paged_value_store.shape, bf16),
        ],
        in_specs=[pl.BlockSpec(memory_space=pltpu.HBM)] * len(given),
        out_specs=[vmem] * replicas + [smem] * 2 + [vmem] * 2,
        scratch_shapes=[
            pltpu.VMEM(queries.shape, bf16),
            pltpu.VMEM(fresh_key_rows.shape, bf16),
            pltpu.VMEM(fresh_value_rows.shape, bf16),
            pltpu.SMEM((rows,), i32),
            pltpu.VMEM((1, rows), i32),
            pltpu.VMEM((1, rows), i32),
            pltpu.VMEM(((rows + 1) * heads, HEAD_SIZE), f32),
            pltpu.VMEM(((rows + 1) * step, HEAD_SIZE), f32),
            pltpu.VMEM((rows + 8, HEAD_SIZE), f32),
            pltpu.VMEM((new_size, HEAD_SIZE), f32),
            pltpu.VMEM((meta_size, HEAD_SIZE), f32),
            pltpu.SMEM((replicas,), i32),
            pltpu.SMEM((replicas,), i32),
            pltpu.SemaphoreType.DMA((len(given),)),
        ],
        compiler_params=params,
        name="pack",
    )(*[pltpu.with_memory_space_constraint(x, pltpu.HBM) for x in given])
    blocks = packed[:replicas]
    slot_rows, table = map(in_smem, packed[replicas : replicas + 2])
    keys, values = map(in_vmem, packed[replicas + 2 :])

    def serve(asked):
        return pl.pallas_call(
            functools.partial(serve_kernel, capacity, heads),
            out_shape=[pltpu.VMEM((capacity * heads, HEAD_SIZE), bf16)] * len(asked),
            in_specs=[smem] + [vmem] * (2 + len(asked)),
            out_specs=[vmem] * len(asked),
            compiler_params=params,
            cost_estimate=pl.CostEstimate(flops=10**7, bytes_accessed=2 * 10**6, transcendentals=0),
            name="serve",
        )(table, keys, values, *map(in_vmem, asked))

    def swap(x, turn):
        cores = lax.axis_size("tensor")
        pairs = [
            (i * cores + core, (i ^ turns[core % 2][turn]) * cores + core)
            for i in range(replicas)
            for core in range(cores)
        ]
        return lax.ppermute(x, ("replica", "tensor"), pairs)

    arrived = [swap(blocks[turn], turn) for turn in range(replicas - 1)] + [blocks[replicas - 1]]
    answers = []
    for turn in range(0, replicas, TOGETHER):
        for answer in serve(arrived[turn : turn + TOGETHER]):
            answers.append(swap(answer, len(answers)) if len(answers) < replicas - 1 else answer)

    attended, partial_reward = pl.pallas_call(
        functools.partial(unpack_kernel, capacity, heads, rows),
        out_shape=[pltpu.VMEM((rows, heads * HEAD_SIZE), bf16), pltpu.VMEM((1, rows), f32)],
        in_specs=[smem] + [vmem] * (replicas + 1),
        out_specs=[vmem] * 2,
        scratch_shapes=[pltpu.VMEM(((rows + 1) * heads, HEAD_SIZE), f32)],
        compiler_params=params,
        name="unpack",
    )(slot_rows, in_vmem(reward_probe.reshape(1, -1)), *[in_vmem(x) for x in answers])
    other_half = lax.ppermute(partial_reward, "tensor", [(0, 1), (1, 0)])
    return attended, (partial_reward + other_half)[0]


def solution(mesh):
    placed = (
        P(("groups", "replica"), "tensor"),
        P(("groups", "replica"), "tensor"),
        P(("groups", "replica"), "tensor"),
        P(("groups", "replica"), None, "tensor"),
        P(("groups", "replica"), None, "tensor"),
        P(("groups", "replica"), None),
        P(("groups", "replica"), None),
        P(("groups", "replica"), None),
        P(("groups", "replica")),
        P("tensor"),
    )
    return jax.shard_map(
        shards,
        mesh=mesh,
        in_specs=placed,
        out_specs=(P(("groups", "replica"), "tensor"), P(("groups", "replica"))),
        check_vma=False,
    )
```

```python
import functools

import jax
import jax.numpy as jnp
from jax import lax
from jax.experimental import pallas as pl
from jax.experimental.pallas import tpu as pltpu
from jax.sharding import PartitionSpec as P

HEAD_SIZE = 128
TILE = 16
masked_score = -1e30
f32, bf16, i32 = jnp.float32, jnp.bfloat16, jnp.int32


def round_up(number, step):
    return -(-number // step) * step


def block_rows(capacity, heads, key_heads):
    return capacity * heads, round_up(capacity * key_heads, TILE), round_up(capacity, TILE)


def iota(shape, axis):
    return lax.broadcasted_iota(i32, shape, axis)


def partners_in_turn(replicas):
    near, far = list(range(1, replicas // 2)), list(range(replicas // 2, replicas))
    other_far = list(far)
    for i in range(1, len(far) - 1, 2):
        other_far[i : i + 2] = other_far[i + 1], other_far[i]
    even = [m for pair in zip(far, near) for m in pair] + far[len(near) :] + [0]
    odd = [m for pair in zip(near, other_far) for m in pair] + other_far[len(near) :] + [0]
    return even, odd


def start_copies(sources, targets, arrived):
    copies = [
        pltpu.make_async_copy(source, target, arrived.at[i])
        for i, (source, target) in enumerate(zip(sources, targets))
    ]
    for copy in copies:
        copy.start()
    return copies


def fill(blocks, capacity, heads, key_heads, row_ref, q_rows, value_rows, facts, new_values, meta):
    q_size, new_size, _ = block_rows(capacity, heads, key_heads)
    step = round_up(key_heads, 8)
    for turn, block in enumerate(blocks):
        for slot in range(capacity):
            row = row_ref[turn * capacity + slot]
            block[slot * heads : (slot + 1) * heads, :] = q_rows[
                pl.ds(pl.multiple_of(row * heads, heads), heads), :
            ].astype(bf16)
            own = value_rows[pl.ds(pl.multiple_of(row * step, step), step), :]
            new_values[slot * key_heads : (slot + 1) * key_heads, :] = own[:key_heads]
            meta[slot : slot + 1, :] = facts[pl.ds(row, 1), :]
        block[q_size : q_size + new_size, :] = new_values[...].astype(bf16)
        block[q_size + new_size :, :] = meta[...].astype(bf16)


def pack_kernel(
    capacity,
    turns,
    q_hbm,
    k_hbm,
    v_hbm,
    source_hbm,
    parent_hbm,
    length_hbm,
    table_hbm,
    key_hbm,
    value_hbm,
    *rest,
):
    replicas = len(turns[0])
    blocks, rest = rest[:replicas], rest[replicas:]
    row_ref, table_ref, keys_ref, values_ref = rest[:4]
    q_ref, k_ref, v_ref, source_ref, parent_ref, length_ref = rest[4:10]
    q_rows, value_rows, facts, new_values, meta, taken, turn_ref, arrived = rest[10:]
    copies = start_copies(
        (source_hbm, q_hbm, k_hbm, v_hbm, parent_hbm, length_hbm, table_hbm, key_hbm, value_hbm),
        (source_ref, q_ref, k_ref, v_ref, parent_ref, length_ref, table_ref, keys_ref, values_ref),
        arrived,
    )
    rows = q_ref.shape[0]
    heads, key_heads = q_ref.shape[1] // HEAD_SIZE, k_ref.shape[1] // HEAD_SIZE
    step = round_up(key_heads, 8)
    me, odd = lax.axis_index("replica"), lax.rem(lax.axis_index("tensor"), 2)
    for slot in range(replicas * capacity):
        row_ref[slot] = rows
    for replica in range(replicas):
        taken[replica] = 0
        even_turn, odd_turn = (turn.index(replica) for turn in turns)
        turn_ref[replica] = jnp.where(odd == 1, odd_turn, even_turn)
    q_rows[rows * heads :, :] = jnp.zeros((heads, HEAD_SIZE), f32)
    value_rows[rows * step :, :] = jnp.zeros((step, HEAD_SIZE), f32)
    facts[rows:, :] = jnp.zeros((facts.shape[0] - rows, HEAD_SIZE), f32)
    new_values[...] = jnp.zeros_like(new_values)
    meta[...] = jnp.zeros_like(meta)
    copies[0].wait()
    for row in range(rows):
        source = source_ref[row]
        rank = taken[source]
        taken[source] = rank + 1
        row_ref[turn_ref[source ^ me] * capacity + rank] = row
    for copy in copies[1:6]:
        copy.wait()
    lane = iota((rows, HEAD_SIZE), 1)
    own = jnp.zeros((rows, HEAD_SIZE), f32)
    for head in range(heads):
        lanes = slice(head * HEAD_SIZE, (head + 1) * HEAD_SIZE)
        q_head = q_ref[:, lanes].astype(f32)
        q_rows[pl.ds(head, rows, stride=heads), :] = q_head
        key_head = head // (heads // key_heads)
        if head % (heads // key_heads) == 0:
            lanes = slice(key_head * HEAD_SIZE, (key_head + 1) * HEAD_SIZE)
            k_head = k_ref[:, lanes].astype(f32)
            value_rows[pl.ds(key_head, rows, stride=step), :] = v_ref[:, lanes].astype(f32)
        score = jnp.sum(q_head * k_head, axis=1, keepdims=True)
        own = jnp.where(lane % heads == head, score, own)
    high = own.astype(bf16).astype(f32)
    middle = (own - high).astype(bf16).astype(f32)
    low = own - high - middle
    part = lane // heads
    own = jnp.where(part == 1, high, jnp.where(part == 2, middle, jnp.where(part == 3, low, 0.0)))
    diagonal = iota((rows, rows), 0) == iota((rows, rows), 1)

    def column(ref):
        return jnp.sum(jnp.where(diagonal, ref[...].astype(f32), 0.0), axis=1, keepdims=True)

    facts[:rows, :] = jnp.where(lane == 0, column(parent_ref), jnp.where(lane == 1, column(length_ref), own))
    fill(blocks, capacity, heads, key_heads, row_ref, q_rows, value_rows, facts, new_values, meta)
    for copy in copies[6:]:
        copy.wait()


def serve_kernel(capacity, heads, table_ref, key_ref, value_ref, *blocks_and_answers):
    number = len(blocks_and_answers) // 2
    blocks, answers = blocks_and_answers[:number], blocks_and_answers[number:]
    pages_per_row, rows = table_ref.shape
    positions, width = key_ref.shape[1:]
    key_heads = width // HEAD_SIZE
    group = heads // key_heads
    span = pages_per_row * positions
    scaling = 1.0 / HEAD_SIZE**0.5
    q_size, new_size, meta_size = block_rows(capacity, heads, key_heads)
    per_tile = TILE // key_heads
    slots = [(n, slot) for n in range(number) for slot in range(capacity)]

    at_row, at_lane = iota((meta_size, HEAD_SIZE), 0), iota((meta_size, HEAD_SIZE), 1)
    metas = [block[q_size + new_size :, :].astype(f32) for block in blocks]
    at_lane_of_head = iota((heads, HEAD_SIZE), 1)
    picked = (at_lane_of_head % heads == iota((heads, HEAD_SIZE), 0)) & (at_lane_of_head >= heads)
    by_lanes = (((1,), (1,)), ((), ()))
    picked = jnp.where(picked, 1.0, 0.0).astype(bf16)
    coded = [jnp.where(at_lane == 0, meta, jnp.where(at_lane == 1, meta * rows, 0.0)) for meta in metas]
    codes = [jnp.sum(jnp.where(at_row == slot, coded[n], 0.0)).astype(i32) for n, slot in slots]
    lengths = [code // rows for code in codes]
    parents = [code - length * rows for code, length in zip(codes, lengths)]
    pages = [[table_ref[i, parent] for i in range(pages_per_row)] for parent in parents]
    diagonal = iota((heads, width), 0) // group == iota((heads, width), 1) // HEAD_SIZE
    own_lane = iota((heads, TILE), 1) - iota((heads, TILE), 0) // group
    seen = iota((heads, span), 1)
    scores, new_scores = [], []
    for (n, slot), found in zip(slots, pages):
        q_slot = blocks[n][slot * heads : (slot + 1) * heads, :]
        keys = jnp.concatenate([key_ref[page] for page in found], axis=0)
        spread = jnp.where(diagonal, jnp.concatenate([q_slot] * key_heads, axis=1), jnp.zeros((), bf16))
        scores.append(lax.dot_general(spread, keys, by_lanes, preferred_element_type=f32))
        parts = jnp.broadcast_to(metas[n][slot : slot + 1, :], (TILE, HEAD_SIZE)).astype(bf16)
        new_scores.append(lax.dot_general(picked, parts, by_lanes, preferred_element_type=f32))
    weights, own_weights, denominators = [], [], []
    for (_, slot), length, score, new_score in zip(slots, lengths, scores, new_scores):
        included = jnp.where(seen < length, score * scaling, masked_score)
        own = jnp.where(own_lane == slot % per_tile * key_heads, new_score * scaling, masked_score)
        peak = jnp.maximum(jnp.max(included, axis=1, keepdims=True), jnp.max(own, axis=1, keepdims=True))
        weight, own_weight = jnp.exp(included - peak), jnp.exp(own - peak)
        denominators.append(
            jnp.sum(weight, axis=1, keepdims=True) + jnp.sum(own_weight, axis=1, keepdims=True)
        )
        weights.append(weight.astype(bf16))
        own_weights.append(own_weight.astype(bf16))
    for i, (n, slot) in enumerate(slots):
        tile = q_size + slot // per_tile * TILE
        own_values = blocks[n][tile : tile + TILE, :]
        values = jnp.concatenate([value_ref[page] for page in pages[i]], axis=0)
        wide = jnp.dot(weights[i], values, preferred_element_type=f32)
        numerator = jnp.concatenate(
            [
                wide[head * group : (head + 1) * group, head * HEAD_SIZE : (head + 1) * HEAD_SIZE]
                for head in range(key_heads)
            ],
            axis=0,
        ) + jnp.dot(own_weights[i], own_values, preferred_element_type=f32)
        answers[n][slot * heads : (slot + 1) * heads, :] = (numerator / denominators[i]).astype(bf16)


def unpack_kernel(capacity, heads, rows, row_ref, probe_ref, *rest):
    answers, (out_ref, reward_ref, gathered) = rest[:-3], rest[-3:]
    for partner, answer in enumerate(answers):
        for slot in range(capacity):
            row = row_ref[partner * capacity + slot]
            gathered[pl.ds(pl.multiple_of(row * heads, heads), heads), :] = answer[
                slot * heads : (slot + 1) * heads, :
            ].astype(f32)
    total = jnp.zeros((rows, HEAD_SIZE), f32)
    for head in range(heads):
        part = gathered[pl.ds(head, rows, stride=heads), :]
        out_ref[:, head * HEAD_SIZE : (head + 1) * HEAD_SIZE] = part.astype(bf16)
        total = total + part * probe_ref[:, head * HEAD_SIZE : (head + 1) * HEAD_SIZE].astype(f32)
    reward_ref[...] = jnp.sum(total.T, axis=0, keepdims=True)


def shards(
    queries,
    fresh_key_rows,
    fresh_value_rows,
    paged_key_store,
    paged_value_store,
    page_table,
    parent_replica,
    parent_slot,
    context_length,
    reward_probe,
):
    replicas = lax.axis_size("replica")
    rows = queries.shape[0]
    capacity = max(2, 2 * rows // replicas)
    heads = queries.shape[1] // HEAD_SIZE
    key_heads = fresh_key_rows.shape[1] // HEAD_SIZE
    q_size, new_size, meta_size = block_rows(capacity, heads, key_heads)
    block_size = q_size + new_size + meta_size
    step = round_up(key_heads, 8)
    vmem, smem = pl.BlockSpec(memory_space=pltpu.VMEM), pl.BlockSpec(memory_space=pltpu.SMEM)
    params = pltpu.CompilerParams(vmem_limit_bytes=16 * 2**20)

    def in_vmem(x):
        return pltpu.with_memory_space_constraint(x, pltpu.VMEM)

    def in_smem(x):
        return pltpu.with_memory_space_constraint(x, pltpu.SMEM)

    turns = partners_in_turn(replicas)
    given = (
        queries,
        fresh_key_rows,
        fresh_value_rows,
        parent_replica[:, 0],
        parent_slot.reshape(1, rows),
        context_length.reshape(1, rows),
        page_table.T,
        paged_key_store,
        paged_value_store,
    )
    packed = pl.pallas_call(
        functools.partial(pack_kernel, capacity, turns),
        out_shape=[pltpu.VMEM((block_size, HEAD_SIZE), bf16)] * replicas
        + [
            pltpu.SMEM((replicas * capacity,), i32),
            pltpu.SMEM(page_table.shape[::-1], i32),
            pltpu.VMEM(paged_key_store.shape, bf16),
            pltpu.VMEM(paged_value_store.shape, bf16),
        ],
        in_specs=[pl.BlockSpec(memory_space=pltpu.HBM)] * len(given),
        out_specs=[vmem] * replicas + [smem] * 2 + [vmem] * 2,
        scratch_shapes=[
            pltpu.VMEM(queries.shape, bf16),
            pltpu.VMEM(fresh_key_rows.shape, bf16),
            pltpu.VMEM(fresh_value_rows.shape, bf16),
            pltpu.SMEM((rows,), i32),
            pltpu.VMEM((1, rows), i32),
            pltpu.VMEM((1, rows), i32),
            pltpu.VMEM(((rows + 1) * heads, HEAD_SIZE), f32),
            pltpu.VMEM(((rows + 1) * step, HEAD_SIZE), f32),
            pltpu.VMEM((rows + 8, HEAD_SIZE), f32),
            pltpu.VMEM((new_size, HEAD_SIZE), f32),
            pltpu.VMEM((meta_size, HEAD_SIZE), f32),
            pltpu.SMEM((replicas,), i32),
            pltpu.SMEM((replicas,), i32),
            pltpu.SemaphoreType.DMA((len(given),)),
        ],
        compiler_params=params,
        name="pack",
    )(*[pltpu.with_memory_space_constraint(x, pltpu.HBM) for x in given])
    blocks = packed[:replicas]
    slot_rows, table = map(in_smem, packed[replicas : replicas + 2])
    keys, values = map(in_vmem, packed[replicas + 2 :])

    def serve(asked):
        return pl.pallas_call(
            functools.partial(serve_kernel, capacity, heads),
            out_shape=[pltpu.VMEM((capacity * heads, HEAD_SIZE), bf16)] * len(asked),
            in_specs=[smem] + [vmem] * (2 + len(asked)),
            out_specs=[vmem] * len(asked),
            compiler_params=params,
            cost_estimate=pl.CostEstimate(flops=10**7, bytes_accessed=2 * 10**6, transcendentals=0),
            name="serve",
        )(table, keys, values, *map(in_vmem, asked))

    def swap(x, turn):
        cores = lax.axis_size("tensor")
        pairs = [
            (i * cores + core, (i ^ turns[core % 2][turn]) * cores + core)
            for i in range(replicas)
            for core in range(cores)
        ]
        return lax.ppermute(x, ("replica", "tensor"), pairs)

    arrived = [swap(blocks[turn], turn) for turn in range(replicas - 1)] + [blocks[replicas - 1]]
    answers = [None] * replicas
    groups = [[0, replicas - 1]] + [[turn, turn + 1] for turn in range(1, replicas - 1, 2)]
    for group in groups:
        for turn, answer in zip(group, serve([arrived[turn] for turn in group])):
            answers[turn] = swap(answer, turn) if turn < replicas - 1 else answer

    attended, partial_reward = pl.pallas_call(
        functools.partial(unpack_kernel, capacity, heads, rows),
        out_shape=[pltpu.VMEM((rows, heads * HEAD_SIZE), bf16), pltpu.VMEM((1, rows), f32)],
        in_specs=[smem] + [vmem] * (replicas + 1),
        out_specs=[vmem] * 2,
        scratch_shapes=[pltpu.VMEM(((rows + 1) * heads, HEAD_SIZE), f32)],
        compiler_params=params,
        name="unpack",
    )(slot_rows, in_vmem(reward_probe.reshape(1, -1)), *[in_vmem(x) for x in answers])
    other_half = lax.ppermute(partial_reward, "tensor", [(0, 1), (1, 0)])
    return attended, (partial_reward + other_half)[0]


def solution(mesh):
    placed = (
        P(("groups", "replica"), "tensor"),
        P(("groups", "replica"), "tensor"),
        P(("groups", "replica"), "tensor"),
        P(("groups", "replica"), None, "tensor"),
        P(("groups", "replica"), None, "tensor"),
        P(("groups", "replica"), None),
        P(("groups", "replica"), None),
        P(("groups", "replica"), None),
        P(("groups", "replica")),
        P("tensor"),
    )
    return jax.shard_map(
        shards,
        mesh=mesh,
        in_specs=placed,
        out_specs=(P(("groups", "replica"), "tensor"), P(("groups", "replica"))),
        check_vma=False,
    )
```

```python
import functools

import jax
import jax.numpy as jnp
from jax import lax
from jax.experimental import pallas as pl
from jax.experimental.pallas import tpu as pltpu
from jax.sharding import PartitionSpec as P

HEAD_SIZE = 128
TILE = 16
masked_score = -1e30
f32, bf16, i32 = jnp.float32, jnp.bfloat16, jnp.int32


def round_up(number, step):
    return -(-number // step) * step


def block_rows(capacity, heads, key_heads):
    return capacity * heads, round_up(capacity * key_heads, TILE), round_up(capacity, TILE)


def iota(shape, axis):
    return lax.broadcasted_iota(i32, shape, axis)


def partners_in_turn(replicas):
    near, far = list(range(1, replicas // 2)), list(range(replicas // 2, replicas))
    other_far = list(far)
    for i in range(1, len(far) - 1, 2):
        other_far[i : i + 2] = other_far[i + 1], other_far[i]
    even = [m for pair in zip(far, near) for m in pair] + far[len(near) :] + [0]
    odd = [m for pair in zip(near, other_far) for m in pair] + other_far[len(near) :] + [0]
    return even, odd


def start_copies(sources, targets, arrived):
    copies = [
        pltpu.make_async_copy(source, target, arrived.at[i])
        for i, (source, target) in enumerate(zip(sources, targets))
    ]
    for copy in copies:
        copy.start()
    return copies


def fill(blocks, capacity, heads, key_heads, row_ref, q_rows, value_rows, facts, new_values, meta):
    q_size, new_size, _ = block_rows(capacity, heads, key_heads)
    step = round_up(key_heads, 8)
    for turn, block in enumerate(blocks):
        for slot in range(capacity):
            row = row_ref[turn * capacity + slot]
            block[slot * heads : (slot + 1) * heads, :] = q_rows[
                pl.ds(pl.multiple_of(row * heads, heads), heads), :
            ].astype(bf16)
            own = value_rows[pl.ds(pl.multiple_of(row * step, step), step), :]
            new_values[slot * key_heads : (slot + 1) * key_heads, :] = own[:key_heads]
            meta[slot : slot + 1, :] = facts[pl.ds(row, 1), :]
        block[q_size : q_size + new_size, :] = new_values[...].astype(bf16)
        block[q_size + new_size :, :] = meta[...].astype(bf16)


def pack_kernel(
    capacity,
    turns,
    q_hbm,
    k_hbm,
    v_hbm,
    source_hbm,
    parent_hbm,
    length_hbm,
    table_hbm,
    key_hbm,
    value_hbm,
    *rest,
):
    replicas = len(turns[0])
    blocks, rest = rest[:replicas], rest[replicas:]
    row_ref, table_ref, keys_ref, values_ref = rest[:4]
    q_ref, k_ref, v_ref, source_ref, parent_ref, length_ref = rest[4:10]
    q_rows, value_rows, facts, new_values, meta, taken, turn_ref, arrived = rest[10:]
    copies = start_copies(
        (source_hbm, q_hbm, k_hbm, v_hbm, parent_hbm, length_hbm, table_hbm, key_hbm, value_hbm),
        (source_ref, q_ref, k_ref, v_ref, parent_ref, length_ref, table_ref, keys_ref, values_ref),
        arrived,
    )
    rows = q_ref.shape[0]
    heads, key_heads = q_ref.shape[1] // HEAD_SIZE, k_ref.shape[1] // HEAD_SIZE
    step = round_up(key_heads, 8)
    me, odd = lax.axis_index("replica"), lax.rem(lax.axis_index("tensor"), 2)
    for slot in range(replicas * capacity):
        row_ref[slot] = rows
    for replica in range(replicas):
        taken[replica] = 0
        even_turn, odd_turn = (turn.index(replica) for turn in turns)
        turn_ref[replica] = jnp.where(odd == 1, odd_turn, even_turn)
    q_rows[rows * heads :, :] = jnp.zeros((heads, HEAD_SIZE), f32)
    value_rows[rows * step :, :] = jnp.zeros((step, HEAD_SIZE), f32)
    facts[rows:, :] = jnp.zeros((facts.shape[0] - rows, HEAD_SIZE), f32)
    new_values[...] = jnp.zeros_like(new_values)
    meta[...] = jnp.zeros_like(meta)
    copies[0].wait()
    for row in range(rows):
        source = source_ref[row]
        rank = taken[source]
        taken[source] = rank + 1
        row_ref[turn_ref[source ^ me] * capacity + rank] = row
    for copy in copies[1:6]:
        copy.wait()
    lane = iota((rows, HEAD_SIZE), 1)
    own = jnp.zeros((rows, HEAD_SIZE), f32)
    for head in range(heads):
        lanes = slice(head * HEAD_SIZE, (head + 1) * HEAD_SIZE)
        q_head = q_ref[:, lanes].astype(f32)
        q_rows[pl.ds(head, rows, stride=heads), :] = q_head
        key_head = head // (heads // key_heads)
        if head % (heads // key_heads) == 0:
            lanes = slice(key_head * HEAD_SIZE, (key_head + 1) * HEAD_SIZE)
            k_head = k_ref[:, lanes].astype(f32)
            value_rows[pl.ds(key_head, rows, stride=step), :] = v_ref[:, lanes].astype(f32)
        score = jnp.sum(q_head * k_head, axis=1, keepdims=True)
        own = jnp.where(lane % heads == head, score, own)
    high = own.astype(bf16).astype(f32)
    middle = (own - high).astype(bf16).astype(f32)
    low = own - high - middle
    part = lane // heads
    own = jnp.where(part == 1, high, jnp.where(part == 2, middle, jnp.where(part == 3, low, 0.0)))
    diagonal = iota((rows, rows), 0) == iota((rows, rows), 1)

    def column(ref):
        return jnp.sum(jnp.where(diagonal, ref[...].astype(f32), 0.0), axis=1, keepdims=True)

    facts[:rows, :] = jnp.where(lane == 0, column(parent_ref), jnp.where(lane == 1, column(length_ref), own))
    fill(blocks, capacity, heads, key_heads, row_ref, q_rows, value_rows, facts, new_values, meta)
    for copy in copies[6:]:
        copy.wait()


def serve_kernel(capacity, heads, table_ref, key_ref, value_ref, *blocks_and_answers):
    number = len(blocks_and_answers) // 2
    blocks, answers = blocks_and_answers[:number], blocks_and_answers[number:]
    pages_per_row, rows = table_ref.shape
    positions, width = key_ref.shape[1:]
    key_heads = width // HEAD_SIZE
    group = heads // key_heads
    span = pages_per_row * positions
    scaling = 1.0 / HEAD_SIZE**0.5
    q_size, new_size, meta_size = block_rows(capacity, heads, key_heads)
    per_tile = TILE // key_heads
    slots = [(n, slot) for n in range(number) for slot in range(capacity)]

    at_row, at_lane = iota((meta_size, HEAD_SIZE), 0), iota((meta_size, HEAD_SIZE), 1)
    metas = [block[q_size + new_size :, :].astype(f32) for block in blocks]
    at_lane_of_head = iota((heads, HEAD_SIZE), 1)
    picked = (at_lane_of_head % heads == iota((heads, HEAD_SIZE), 0)) & (at_lane_of_head >= heads)
    by_lanes = (((1,), (1,)), ((), ()))
    picked = jnp.where(picked, 1.0, 0.0).astype(bf16)
    coded = [jnp.where(at_lane == 0, meta, jnp.where(at_lane == 1, meta * rows, 0.0)) for meta in metas]
    codes = [jnp.sum(jnp.where(at_row == slot, coded[n], 0.0)).astype(i32) for n, slot in slots]
    lengths = [code // rows for code in codes]
    parents = [code - length * rows for code, length in zip(codes, lengths)]
    pages = [[table_ref[i, parent] for i in range(pages_per_row)] for parent in parents]
    diagonal = iota((heads, width), 0) // group == iota((heads, width), 1) // HEAD_SIZE
    own_lane = iota((heads, TILE), 1) - iota((heads, TILE), 0) // group
    seen = iota((heads, span), 1)
    scores, new_scores = [], []
    for (n, slot), found in zip(slots, pages):
        q_slot = blocks[n][slot * heads : (slot + 1) * heads, :]
        keys = jnp.concatenate([key_ref[page] for page in found], axis=0)
        spread = jnp.where(diagonal, jnp.concatenate([q_slot] * key_heads, axis=1), jnp.zeros((), bf16))
        scores.append(lax.dot_general(spread, keys, by_lanes, preferred_element_type=f32))
        parts = jnp.broadcast_to(metas[n][slot : slot + 1, :], (TILE, HEAD_SIZE)).astype(bf16)
        new_scores.append(lax.dot_general(picked, parts, by_lanes, preferred_element_type=f32))
    weights, own_weights, denominators = [], [], []
    for (_, slot), length, score, new_score in zip(slots, lengths, scores, new_scores):
        included = jnp.where(seen < length, score * scaling, masked_score)
        own = jnp.where(own_lane == slot % per_tile * key_heads, new_score * scaling, masked_score)
        peak = jnp.maximum(jnp.max(included, axis=1, keepdims=True), jnp.max(own, axis=1, keepdims=True))
        weight, own_weight = jnp.exp(included - peak), jnp.exp(own - peak)
        denominators.append(
            jnp.sum(weight, axis=1, keepdims=True) + jnp.sum(own_weight, axis=1, keepdims=True)
        )
        weights.append(weight.astype(bf16))
        own_weights.append(own_weight.astype(bf16))
    for i, (n, slot) in enumerate(slots):
        tile = q_size + slot // per_tile * TILE
        own_values = blocks[n][tile : tile + TILE, :]
        values = jnp.concatenate([value_ref[page] for page in pages[i]], axis=0)
        wide = jnp.dot(weights[i], values, preferred_element_type=f32)
        numerator = jnp.concatenate(
            [
                wide[head * group : (head + 1) * group, head * HEAD_SIZE : (head + 1) * HEAD_SIZE]
                for head in range(key_heads)
            ],
            axis=0,
        ) + jnp.dot(own_weights[i], own_values, preferred_element_type=f32)
        answers[n][slot * heads : (slot + 1) * heads, :] = (numerator / denominators[i]).astype(bf16)


def gather_kernel(capacity, heads, turns, row_ref, *rest):
    answers, gathered = rest[: len(turns)], rest[-1]
    for turn, answer in zip(turns, answers):
        for slot in range(capacity):
            row = row_ref[turn * capacity + slot]
            gathered[pl.ds(pl.multiple_of(row * heads, heads), heads), :] = answer[
                slot * heads : (slot + 1) * heads, :
            ].astype(f32)


def unpack_kernel(capacity, heads, rows, turns, row_ref, probe_ref, *rest):
    answers, (_, out_ref, reward_ref, gathered) = rest[: len(turns)], rest[len(turns) :]
    gather_kernel(capacity, heads, turns, row_ref, *answers, gathered)
    total = jnp.zeros((rows, HEAD_SIZE), f32)
    for head in range(heads):
        part = gathered[pl.ds(head, rows, stride=heads), :]
        out_ref[:, head * HEAD_SIZE : (head + 1) * HEAD_SIZE] = part.astype(bf16)
        total = total + part * probe_ref[:, head * HEAD_SIZE : (head + 1) * HEAD_SIZE].astype(f32)
    reward_ref[...] = jnp.sum(total.T, axis=0, keepdims=True)


def shards(
    queries,
    fresh_key_rows,
    fresh_value_rows,
    paged_key_store,
    paged_value_store,
    page_table,
    parent_replica,
    parent_slot,
    context_length,
    reward_probe,
):
    replicas = lax.axis_size("replica")
    rows = queries.shape[0]
    capacity = max(2, 2 * rows // replicas)
    heads = queries.shape[1] // HEAD_SIZE
    key_heads = fresh_key_rows.shape[1] // HEAD_SIZE
    q_size, new_size, meta_size = block_rows(capacity, heads, key_heads)
    block_size = q_size + new_size + meta_size
    step = round_up(key_heads, 8)
    vmem, smem = pl.BlockSpec(memory_space=pltpu.VMEM), pl.BlockSpec(memory_space=pltpu.SMEM)
    params = pltpu.CompilerParams(vmem_limit_bytes=16 * 2**20)

    def in_vmem(x):
        return pltpu.with_memory_space_constraint(x, pltpu.VMEM)

    def in_smem(x):
        return pltpu.with_memory_space_constraint(x, pltpu.SMEM)

    turns = partners_in_turn(replicas)
    given = (
        queries,
        fresh_key_rows,
        fresh_value_rows,
        parent_replica[:, 0],
        parent_slot.reshape(1, rows),
        context_length.reshape(1, rows),
        page_table.T,
        paged_key_store,
        paged_value_store,
    )
    packed = pl.pallas_call(
        functools.partial(pack_kernel, capacity, turns),
        out_shape=[pltpu.VMEM((block_size, HEAD_SIZE), bf16)] * replicas
        + [
            pltpu.SMEM((replicas * capacity,), i32),
            pltpu.SMEM(page_table.shape[::-1], i32),
            pltpu.VMEM(paged_key_store.shape, bf16),
            pltpu.VMEM(paged_value_store.shape, bf16),
        ],
        in_specs=[pl.BlockSpec(memory_space=pltpu.HBM)] * len(given),
        out_specs=[vmem] * replicas + [smem] * 2 + [vmem] * 2,
        scratch_shapes=[
            pltpu.VMEM(queries.shape, bf16),
            pltpu.VMEM(fresh_key_rows.shape, bf16),
            pltpu.VMEM(fresh_value_rows.shape, bf16),
            pltpu.SMEM((rows,), i32),
            pltpu.VMEM((1, rows), i32),
            pltpu.VMEM((1, rows), i32),
            pltpu.VMEM(((rows + 1) * heads, HEAD_SIZE), f32),
            pltpu.VMEM(((rows + 1) * step, HEAD_SIZE), f32),
            pltpu.VMEM((rows + 8, HEAD_SIZE), f32),
            pltpu.VMEM((new_size, HEAD_SIZE), f32),
            pltpu.VMEM((meta_size, HEAD_SIZE), f32),
            pltpu.SMEM((replicas,), i32),
            pltpu.SMEM((replicas,), i32),
            pltpu.SemaphoreType.DMA((len(given),)),
        ],
        compiler_params=params,
        name="pack",
    )(*[pltpu.with_memory_space_constraint(x, pltpu.HBM) for x in given])
    blocks = packed[:replicas]
    slot_rows, table = map(in_smem, packed[replicas : replicas + 2])
    keys, values = map(in_vmem, packed[replicas + 2 :])

    def serve(asked):
        return pl.pallas_call(
            functools.partial(serve_kernel, capacity, heads),
            out_shape=[pltpu.VMEM((capacity * heads, HEAD_SIZE), bf16)] * len(asked),
            in_specs=[smem] + [vmem] * (2 + len(asked)),
            out_specs=[vmem] * len(asked),
            compiler_params=params,
            cost_estimate=pl.CostEstimate(flops=10**7, bytes_accessed=2 * 10**6, transcendentals=0),
            name="serve",
        )(table, keys, values, *map(in_vmem, asked))

    def swap(x, turn):
        cores = lax.axis_size("tensor")
        pairs = [
            (i * cores + core, (i ^ turns[core % 2][turn]) * cores + core)
            for i in range(replicas)
            for core in range(cores)
        ]
        return lax.ppermute(x, ("replica", "tensor"), pairs)

    arrived = [swap(blocks[turn], turn) for turn in range(replicas - 1)] + [blocks[replicas - 1]]
    answers = [None] * replicas
    groups = [[0, replicas - 1]] + [[turn, turn + 1] for turn in range(1, replicas - 1, 2)]
    for group in groups:
        for turn, answer in zip(group, serve([arrived[turn] for turn in group])):
            answers[turn] = swap(answer, turn) if turn < replicas - 1 else answer

    gathered = pltpu.VMEM(((rows + 1) * heads, HEAD_SIZE), f32)
    last = [0, 1]
    early = [turn for turn in range(replicas) if turn not in last]
    rows_of_early = pl.pallas_call(
        functools.partial(gather_kernel, capacity, heads, early),
        out_shape=gathered,
        in_specs=[smem] + [vmem] * len(early),
        out_specs=vmem,
        compiler_params=params,
        name="gather",
    )(slot_rows, *[in_vmem(answers[turn]) for turn in early])
    attended, partial_reward, _ = pl.pallas_call(
        functools.partial(unpack_kernel, capacity, heads, rows, last),
        out_shape=[pltpu.VMEM((rows, heads * HEAD_SIZE), bf16), pltpu.VMEM((1, rows), f32), gathered],
        in_specs=[smem] + [vmem] * (len(last) + 2),
        out_specs=[vmem] * 3,
        input_output_aliases={len(last) + 2: 2},
        compiler_params=params,
        name="unpack",
    )(
        slot_rows,
        in_vmem(reward_probe.reshape(1, -1)),
        *[in_vmem(answers[turn]) for turn in last],
        in_vmem(rows_of_early),
    )
    other_half = lax.ppermute(partial_reward, "tensor", [(0, 1), (1, 0)])
    return attended, (partial_reward + other_half)[0]


def solution(mesh):
    placed = (
        P(("groups", "replica"), "tensor"),
        P(("groups", "replica"), "tensor"),
        P(("groups", "replica"), "tensor"),
        P(("groups", "replica"), None, "tensor"),
        P(("groups", "replica"), None, "tensor"),
        P(("groups", "replica"), None),
        P(("groups", "replica"), None),
        P(("groups", "replica"), None),
        P(("groups", "replica")),
        P("tensor"),
    )
    return jax.shard_map(
        shards,
        mesh=mesh,
        in_specs=placed,
        out_specs=(P(("groups", "replica"), "tensor"), P(("groups", "replica"))),
        check_vma=False,
    )
```
